128 devices in a mesh: frame: 16 (over z_hi, y, core), row: 8 (over z_lo, x).
Axes of the slice: x: 4, y: 4, z: 4 (z_hi: 2, z_lo: 2; z = z_hi * 2 + z_lo), core: 2. Of those that a mesh axis runs over, the one named last changes fastest.
Arguments:
- latent: bfloat16 [16, 32, 64, 1152], P('frame', 'row'), may hold values from -1.5 to 1.5
- latent_tangent: bfloat16 [16, 32, 64, 1152], P('frame', 'row'), may hold values from -1.5 to 1.5
- modulation: float32 [3, 1152], replicated, may hold values from -3 to 3
- modulation_tangent: float32 [3, 1152], replicated, may hold values from -3 to 3
- w_qkv_s: bfloat16 [1152, 3456], replicated, may hold values from -0.1875 to 0.1875
- w_out_s: bfloat16 [1152, 1152], replicated, may hold values from -0.1875 to 0.1875
- q_gain_s: float32 [72], replicated, may hold values from 0.5 to 3
- k_gain_s: float32 [72], replicated, may hold values from 0.5 to 3
- w_qkv_t: bfloat16 [1152, 3456], replicated, may hold values from -0.1875 to 0.1875
- w_out_t: bfloat16 [1152, 1152], replicated, may hold values from -0.1875 to 0.1875
- q_gain_t: float32 [72], replicated, may hold values from 0.5 to 3
- k_gain_t: float32 [72], replicated, may hold values from 0.5 to 3
Outputs:
- output: bfloat16 [16, 32, 64, 1152], P('frame', 'row')
- output_tangent: bfloat16 [16, 32, 64, 1152], P('frame', 'row')
The draws below stay inside these ranges and needn't reach their ends.
All inputs are finite; a program needn't handle non-finite values.
Results may differ from the reference program's by a relative error of at most 0.033.
Values may be sent and summed in bfloat16 or wider, within the bound.
A program may use at most 128 MiB of HBM per device.

```python
import math
import jax
import jax.numpy as jnp
from jax import lax

D = 1152
HEADS = 16
HEAD_DIM = 72
COLS = 64
ROWS = 32
FRAMES = 16


def draw_q_gain_s(key, part):
    key = jax.random.fold_in(key, 11)
    return jax.random.uniform(key, (HEAD_DIM,), jnp.float32, 1.2, 2.4)


def draw_k_gain_s(key, part):
    key = jax.random.fold_in(key, 23)
    return jax.random.uniform(key, (HEAD_DIM,), jnp.float32, 1.2, 2.4)


def draw_q_gain_t(key, part):
    key = jax.random.fold_in(key, 37)
    return jax.random.uniform(key, (HEAD_DIM,), jnp.float32, 1.2, 2.4)


def draw_k_gain_t(key, part):
    key = jax.random.fold_in(key, 41)
    return jax.random.uniform(key, (HEAD_DIM,), jnp.float32, 1.2, 2.4)


def block_levels(rng, dims, cuts, least, high):
    level, own = 1.0, jax.random.fold_in(rng, 6)
    for dim, blocks in cuts:
        steps = jnp.exp(jax.random.uniform(jax.random.fold_in(own, dim), (blocks,), jnp.float32, least / len(cuts), high / len(cuts)))
        level = level * jnp.repeat(steps, dims[dim] // blocks).reshape([-1 if axis == dim else 1 for axis in range(len(dims))])
    return level


def noise(rng, shape, deviation, reach, cuts=(), dtype=jnp.bfloat16):
    values = deviation * jax.random.normal(rng, shape, jnp.float32)
    if cuts:
        values = values * block_levels(rng, shape, cuts, -0.22, 0.18)
    return jnp.clip(values, -reach, reach).astype(dtype)


def setup_inputs(seed: int = 0) -> dict:
    arg_keys = jax.random.split(jax.random.key(seed), 13)
    return {
        "latent": noise(arg_keys[0], (FRAMES, ROWS, COLS, D), 0.25, 1.5, ((0, 16), (1, 8))),
        "latent_tangent": noise(arg_keys[1], (FRAMES, ROWS, COLS, D), 0.25, 1.5, ((0, 16), (1, 8))),
        "modulation": noise(arg_keys[2], (3, D), 0.5, 3.0, (), jnp.float32),
        "modulation_tangent": noise(arg_keys[3], (3, D), 0.5, 3.0, (), jnp.float32),
        "w_qkv_s": noise(arg_keys[4], (D, 3 * D), D ** -0.5, 0.1875),
        "w_out_s": noise(arg_keys[5], (D, D), D ** -0.5, 0.1875),
        "q_gain_s": draw_q_gain_s(jax.random.fold_in(arg_keys[12], 71), 0),
        "k_gain_s": draw_k_gain_s(jax.random.fold_in(arg_keys[12], 71), 0),
        "w_qkv_t": noise(arg_keys[8], (D, 3 * D), D ** -0.5, 0.1875),
        "w_out_t": noise(arg_keys[9], (D, D), D ** -0.5, 0.1875),
        "q_gain_t": draw_q_gain_t(jax.random.fold_in(arg_keys[12], 71), 0),
        "k_gain_t": draw_k_gain_t(jax.random.fold_in(arg_keys[12], 71), 0),
    }


EPS = 1e-06

def layer_norm(z, dz):
    zf = z.astype(jnp.float32)
    dzf = dz.astype(jnp.float32)
    cent = zf - lax.optimization_barrier(jnp.mean(zf, -1, keepdims=True))
    rstd = lax.rsqrt(lax.optimization_barrier(jnp.mean(cent * cent, -1, keepdims=True)) + EPS)
    normed = cent * rstd
    dcent = dzf - lax.optimization_barrier(jnp.mean(dzf, -1, keepdims=True))
    dnormed = rstd * (dcent - normed * lax.optimization_barrier(jnp.mean(normed * dcent, -1, keepdims=True)))
    return (normed, dnormed)

def modulate(z, dz, modulation, modulation_tangent):
    normed, dnormed = layer_norm(z, dz)
    hidden = normed * (1.0 + modulation[1]) + modulation[0]
    dhidden = dnormed * (1.0 + modulation[1]) + normed * modulation_tangent[1] + modulation_tangent[0]
    return (hidden.astype(jnp.bfloat16), dhidden.astype(jnp.bfloat16))

def head_norm(value, dvalue, gain):
    rstd = lax.rsqrt(lax.optimization_barrier(jnp.mean(value * value, -1, keepdims=True)) + EPS)
    unit = value * rstd
    inner = dvalue - unit * lax.optimization_barrier(jnp.mean(unit * dvalue, -1, keepdims=True))
    return ((unit * gain).astype(jnp.bfloat16), (gain * rstd * inner).astype(jnp.bfloat16))

def project(hidden, dhidden, w_qkv, q_gain, k_gain, heads):
    width = hidden.shape[1]
    count = hidden.shape[0]
    qkv = jnp.dot(hidden, w_qkv, preferred_element_type=jnp.float32)
    dqkv = jnp.dot(dhidden, w_qkv, preferred_element_type=jnp.float32)

    def split(whole, index):
        return whole[:, index * width:(index + 1) * width].reshape(count, heads, width // heads)
    query, dquery = head_norm(split(qkv, 0), split(dqkv, 0), q_gain)
    keys, dkeys = head_norm(split(qkv, 1), split(dqkv, 1), k_gain)
    values = split(qkv, 2).astype(jnp.bfloat16)
    dvalues = split(dqkv, 2).astype(jnp.bfloat16)
    return (query, keys, values, dquery, dkeys, dvalues)

def attend(query, keys, values, dquery, dkeys, dvalues):
    query, keys, values, dquery, dkeys, dvalues = lax.optimization_barrier((query, keys, values, dquery, dkeys, dvalues))
    query, keys, values, dquery, dkeys, dvalues = [a.astype(jnp.float32) for a in (query, keys, values, dquery, dkeys, dvalues)]
    factor = 1.0 / math.sqrt(query.shape[-1])
    scores = jnp.einsum('qbhe,kbhe->bhqk', query, keys) * factor
    dscores = (jnp.einsum('qbhe,kbhe->bhqk', dquery, keys) + jnp.einsum('qbhe,kbhe->bhqk', query, dkeys)) * factor
    expo = jnp.exp(scores - lax.optimization_barrier(jnp.max(scores, -1, keepdims=True)))
    prob = expo / lax.optimization_barrier(jnp.sum(expo, -1, keepdims=True))
    dprob = prob * (dscores - lax.optimization_barrier(jnp.sum(prob * dscores, -1, keepdims=True)))
    weights = lax.optimization_barrier(prob.astype(jnp.bfloat16)).astype(jnp.float32)
    dweights = lax.optimization_barrier(dprob.astype(jnp.bfloat16)).astype(jnp.float32)
    attn = jnp.einsum('bhqk,kbhe->qbhe', weights, values)
    dattn = jnp.einsum('bhqk,kbhe->qbhe', dweights, values) + jnp.einsum('bhqk,kbhe->qbhe', weights, dvalues)
    return (attn.astype(jnp.bfloat16), dattn.astype(jnp.bfloat16))

def finish(z, dz, attn, dattn, w_out, modulation, modulation_tangent):
    proj = jnp.dot(attn, w_out, preferred_element_type=jnp.float32)
    dproj = jnp.dot(dattn, w_out, preferred_element_type=jnp.float32)
    result = z.astype(jnp.float32) + modulation[2] * proj
    dresult = dz.astype(jnp.float32) + modulation[2] * dproj + modulation_tangent[2] * proj
    return (result.astype(jnp.bfloat16), dresult.astype(jnp.bfloat16))

def reference(latent, latent_tangent, modulation, modulation_tangent, w_qkv_s, w_out_s, q_gain_s, k_gain_s, w_qkv_t, w_out_t, q_gain_t, k_gain_t):
    frames, rows, cols, width = latent.shape
    seq = rows * cols
    tokens = latent.reshape(frames, seq, width)
    dtokens = latent_tangent.reshape(frames, seq, width)

    def spatial_frame(pair):
        ztok, dztok = pair
        hidden, dhidden = modulate(ztok, dztok, modulation, modulation_tangent)
        parts = project(hidden, dhidden, w_qkv_s, q_gain_s, k_gain_s, HEADS)
        heads_first = tuple((jnp.moveaxis(p, 1, 0) for p in parts))

        def one_head(group):
            return attend(*[p[:, None, None, :] for p in group])
        attn, dattn = lax.map(one_head, heads_first)
        attn = jnp.moveaxis(attn.reshape(HEADS, seq, -1), 0, 1).reshape(seq, width)
        dattn = jnp.moveaxis(dattn.reshape(HEADS, seq, -1), 0, 1).reshape(seq, width)
        return finish(ztok, dztok, attn, dattn, w_out_s, modulation, modulation_tangent)
    spatial, dspatial = lax.map(spatial_frame, (tokens, dtokens))
    block = math.gcd(seq, 256)
    nblocks = seq // block
    spatial = jnp.moveaxis(spatial.reshape(frames, nblocks, block, width), 1, 0)
    dspatial = jnp.moveaxis(dspatial.reshape(frames, nblocks, block, width), 1, 0)

    def temporal_block(pair):
        ztok, dztok = pair
        flat = ztok.reshape(frames * block, width)
        dflat = dztok.reshape(frames * block, width)
        hidden, dhidden = modulate(flat, dflat, modulation, modulation_tangent)
        parts = project(hidden, dhidden, w_qkv_t, q_gain_t, k_gain_t, HEADS)
        parts = [p.reshape(frames, block, HEADS, width // HEADS) for p in parts]
        attn, dattn = attend(*parts)
        result, dresult = finish(flat, dflat, attn.reshape(frames * block, width), dattn.reshape(frames * block, width), w_out_t, modulation, modulation_tangent)
        return (result.reshape(frames, block, width), dresult.reshape(frames, block, width))
    output, output_tangent = lax.map(temporal_block, (spatial, dspatial))
    output = jnp.moveaxis(output, 0, 1).reshape(frames, rows, cols, width)
    output_tangent = jnp.moveaxis(output_tangent, 0, 1).reshape(frames, rows, cols, width)
    return (output, output_tangent)
```

```python
import functools
import math

import jax
import jax.numpy as jnp
from jax import lax
from jax.experimental import pallas as pl
from jax.experimental.pallas import tpu as pltpu
from jax.sharding import Mesh, PartitionSpec as P

D = 1152
HEADS = 16
HD = 72
EPS = 1e-06
AXES = ("zh", "y", "core", "zl", "x")
TOK = 256
HALF = 8
FACTOR = 1.0 / math.sqrt(HD)
LOG2E = 1.4426950408889634
MESH = pl.DeviceIdType.MESH
F32 = jnp.float32
BF16 = jnp.bfloat16


def coords():
    return tuple(lax.axis_index(a) for a in AXES)


def dot(a, b, dims):
    return lax.dot_general(a, b, (dims, ((), ())), preferred_element_type=F32)


def normed_hidden(z_of, dz_of, mod_ref, dmod_ref, put):
    rows = 32

    def step(i, _):
        at = pl.multiple_of(i * rows, rows)
        z = z_of(at, rows).astype(F32)
        dz = dz_of(at, rows).astype(F32)
        cent = z - jnp.mean(z, -1, keepdims=True)
        rstd = lax.rsqrt(jnp.mean(cent * cent, -1, keepdims=True) + EPS)
        normed = cent * rstd
        dcent = dz - jnp.mean(dz, -1, keepdims=True)
        dnormed = rstd * (dcent - normed * jnp.mean(normed * dcent, -1, keepdims=True))
        scale = 1.0 + mod_ref[1:2, :]
        hidden = normed * scale + mod_ref[0:1, :]
        dhidden = dnormed * scale + normed * dmod_ref[1:2, :] + dmod_ref[0:1, :]
        put(at, rows, hidden.astype(BF16), dhidden.astype(BF16))
        return 0

    lax.fori_loop(0, TOK // rows, step, 0)


def head_norm(u, du):
    r = lax.rsqrt(jnp.mean(u * u, 0, keepdims=True) + EPS)
    unit = u * r
    return unit, r * (du - unit * jnp.mean(unit * du, 0, keepdims=True))


def query_operands(q, dq, gain):
    unit, inner = head_norm(q, dq)
    qn = unit * (gain * FACTOR)
    dqn = inner * (gain * FACTOR)
    first = jnp.concatenate([qn * LOG2E, jnp.zeros_like(qn)], 0).astype(BF16)
    second = jnp.concatenate([dqn, qn], 0).astype(BF16)
    return first, second


def key_operand(k, dk, gain):
    unit, inner = head_norm(k, dk)
    both = jnp.concatenate([unit * gain, inner * gain], 0)
    return both.T.astype(BF16)


def value_operands(v, dv):
    n = v.shape[1]
    row16 = lax.broadcasted_iota(jnp.int32, (16, n), 0)
    row8 = lax.broadcasted_iota(jnp.int32, (8, n), 0)
    for_e = jnp.concatenate([v, dv, (row16 == 0).astype(F32)], 0).astype(BF16)
    for_g = jnp.concatenate([v, (row8 == 1).astype(F32)], 0).astype(BF16)
    return for_e, for_g


def normalised(acc):
    inv = 1.0 / acc[144:145]
    attn = acc[0:72] * inv
    dattn = (acc[72:144] - acc[145:146] * attn) * inv
    return attn, dattn


def spatial_kernel(
    z_ref, dz_ref, mod_ref, dmod_ref, wqkv_ref, wout_ref, qg_ref, kg_ref,
    out_ref,
    hb, zb, win, wtmp, wt, wout, kt, qs, qd, acc, mx, at, mine, theirs,
    wsem, ro, rb, rz, rx, ss,
):
    zh, y, c, zl, x = coords()
    right = (zh, y, c, zl, lax.rem(x + 1, 4))
    left = (zh, y, c, zl, lax.rem(x + 3, 4))
    sib = (zh, y, 1 - c, zl, x)
    partner = (zh, y, zl, c, x)
    t = lax.rem(c + zl, 2)

    barrier = pltpu.get_barrier_semaphore()
    for peer in (right, left, sib):
        pl.semaphore_signal(barrier, inc=1, device_id=peer, device_id_type=MESH)

    @pl.when(t == 1)
    def _():
        pl.semaphore_signal(barrier, inc=1, device_id=partner, device_id_type=MESH)

    wcopies = [
        pltpu.make_async_copy(
            wqkv_ref.at[:, pl.ds(pl.multiple_of(D * j + 512 * c, 128), 640)], win.at[j], wsem.at[j]
        )
        for j in range(3)
    ] + [pltpu.make_async_copy(wout_ref, wout, wsem.at[3])]
    for copy in wcopies:
        copy.start()

    own = 8 * t

    def put(at_row, rows, h, dh):
        hb[own, 0, pl.ds(at_row, rows), :] = h
        hb[own, 1, pl.ds(at_row, rows), :] = dh

    normed_hidden(
        lambda a, n: z_ref[pl.ds(a, n), :], lambda a, n: dz_ref[pl.ds(a, n), :], mod_ref, dmod_ref, put
    )

    def remote(src, dst, send, recv, to):
        return pltpu.make_async_remote_copy(
            src_ref=src, dst_ref=dst, send_sem=send, recv_sem=recv, device_id=to, device_id_type=MESH
        )

    def slot(dx):
        return hb.at[2 * dx + t]

    to_right = remote(slot(0), slot(3), ss.at[0], ro.at[3], right)
    to_left = remote(slot(0), slot(1), ss.at[1], ro.at[1], left)
    to_sib = [remote(slot(dx), slot(dx), ss.at[2 + dx], rb.at[dx], sib) for dx in range(4)]
    on_left = remote(slot(1).at[0], slot(2).at[0], ss.at[6], ro.at[2], left)
    on_right = remote(slot(3).at[1], slot(2).at[1], ss.at[7], ro.at[4], right)
    swap = remote(hb.at[8], hb.at[1], ss.at[8], ro.at[0], partner)
    swap_z = remote(z_ref, zb.at[0], ss.at[9], rz.at[0], partner)
    swap_dz = remote(dz_ref, zb.at[1], ss.at[10], rz.at[1], partner)

    @pl.when(t == 0)
    def _():
        pl.semaphore_wait(barrier, 3)
        to_sib[0].start()
        to_right.start()
        to_left.start()

    @pl.when(t == 1)
    def _():
        pl.semaphore_wait(barrier, 4)
        swap.start()
        swap_z.start()
        swap_dz.start()

    for j in range(3):
        wcopies[j].wait()
        for i in range(5):
            wtmp[pl.ds(128 * i, 128), :] = win[j, :, pl.ds(128 * i, 128)].T
        wt[pl.ds(576 * j, 576), :] = wtmp[pl.ds(pl.multiple_of(64 * c, 64), 576), :]

    acc[...] = jnp.zeros_like(acc)
    mx[...] = jnp.full_like(mx, -1e30)

    @pl.when(t == 1)
    def _():
        swap.wait_recv()
        to_sib[0].start()
        to_right.start()
        to_left.start()

    to_sib[0].wait_recv()

    for part in range(2):
        h2 = hb[part].reshape(2 * TOK, D)
        kt[0:576, :] = dot(wt[0:576, :], h2, ((1,), (1,)))

        def make_query(h, _):
            at_row = pl.multiple_of(h * HD, 8)
            first, second = query_operands(
                kt[pl.ds(at_row, HD), 0:TOK], kt[pl.ds(at_row, HD), TOK : 2 * TOK], qg_ref[...]
            )
            qs[h, :, TOK * part : TOK * (part + 1)] = first
            qd[h, :, TOK * part : TOK * (part + 1)] = second
            return 0

        lax.fori_loop(0, HALF, make_query, 0)

    def one_shard(i, _):
        late = i >= 6
        tt = jnp.where(late, i - 6, i // 3)
        j = lax.rem(i, 3)
        dx = jnp.where(late, 2, j + j // 2)
        is_own = tt == t

        @pl.when(is_own & (dx == 1))
        def _():
            to_left.wait_recv()
            on_left.start()
            to_sib[1].start()

        @pl.when(is_own & (dx == 3))
        def _():
            to_right.wait_recv()
            on_right.start()
            to_sib[3].start()

        @pl.when(is_own & (dx == 2))
        def _():
            on_left.wait_recv()
            on_right.wait_recv()
            to_sib[2].start()

        for n in (1, 2, 3):
            @pl.when((tt != t) & (dx == n))
            def _():
                to_sib[n].wait_recv()

        index = 2 * dx + tt

        def project(n, _):
            rows = pl.ds(pl.multiple_of(n * 288, 16), 288)
            h2 = hb[index].reshape(2 * TOK, D)
            kt[rows, :] = dot(wt[pl.ds(pl.multiple_of(576 + n * 288, 16), 288), :], h2, ((1,), (1,)))
            return 0

        lax.fori_loop(0, 4, project, 0)

        def one_head(h, _):
            krow = pl.ds(pl.multiple_of(h * HD, 8), HD)
            vrow = pl.ds(pl.multiple_of(576 + h * HD, 8), HD)
            kd = key_operand(kt[krow, 0:TOK], kt[krow, TOK : 2 * TOK], kg_ref[...])
            ve, vg = value_operands(kt[vrow, 0:TOK], kt[vrow, TOK : 2 * TOK])
            s = dot(kd, qs[h], ((1,), (0,)))
            ds = dot(kd, qd[h], ((1,), (0,)))
            old = mx[h, 0:1, :]
            new = jnp.maximum(old, jnp.max(s, 0, keepdims=True))
            mx[h, 0:1, :] = new
            e = jnp.exp2(s - new)
            g = e * ds
            acc[h] = acc[h] * jnp.exp2(old - new) + dot(ve, e.astype(BF16), ((1,), (0,)))
            acc[h, 72:152, :] += dot(vg, g.astype(BF16), ((1,), (0,)))
            return 0

        lax.fori_loop(0, HALF, one_head, 0)
        return 0

    lax.fori_loop(0, 8, one_shard, 0)

    def finish_head(h, _):
        attn, dattn = normalised(acc[h])
        rows = pl.ds(pl.multiple_of(h * HD, 8), HD)
        for part in range(2):
            at[part, 0, rows, :] = attn[:, TOK * part : TOK * (part + 1)]
            at[part, 1, rows, :] = dattn[:, TOK * part : TOK * (part + 1)]
        return 0

    lax.fori_loop(0, HALF, finish_head, 0)
    mine[1] = at[1 - t].astype(BF16)
    trade = remote(mine.at[1], theirs, ss.at[11], rx.at[0], sib)
    trade.start()
    mine[0] = at[t].astype(BF16)
    wcopies[3].wait()
    lo = pl.ds(pl.multiple_of(576 * c, 16), 576)
    hi = pl.ds(pl.multiple_of(576 * (1 - c), 16), 576)
    proj = dot(mine[0, 0], wout[lo, :], ((0,), (0,)))
    dproj = dot(mine[0, 1], wout[lo, :], ((0,), (0,)))
    trade.wait_recv()
    proj += dot(theirs[0], wout[hi, :], ((0,), (0,)))
    dproj += dot(theirs[1], wout[hi, :], ((0,), (0,)))

    @pl.when(t == 0)
    def _():
        zb[0] = z_ref[...]
        zb[1] = dz_ref[...]

    @pl.when(t == 1)
    def _():
        swap_z.wait_recv()
        swap_dz.wait_recv()

    gate = mod_ref[2:3, :]
    dgate = dmod_ref[2:3, :]
    out_ref[:, 0] = (zb[0].astype(F32) + gate * proj).astype(BF16).reshape(16, 16, D)
    out_ref[:, 1] = (zb[1].astype(F32) + gate * dproj + dgate * proj).astype(BF16).reshape(16, 16, D)

    for copy in (to_right, to_left, *to_sib, on_left, on_right, trade):
        copy.wait_send()

    @pl.when(t == 1)
    def _():
        for copy in (swap, swap_z, swap_dz):
            copy.wait_send()


def spatial(z, dz, mod, dmod, wqkv, wout, qg, kg):
    vmem = pl.BlockSpec(memory_space=pltpu.VMEM)
    hbm = pl.BlockSpec(memory_space=pl.ANY)
    dma = pltpu.SemaphoreType.DMA
    return pl.pallas_call(
        spatial_kernel,
        out_shape=jax.ShapeDtypeStruct((16, 2, 16, D), BF16),
        in_specs=[vmem, vmem, vmem, vmem, hbm, hbm, vmem, vmem],
        out_specs=vmem,
        scratch_shapes=[
            pltpu.VMEM((9, 2, TOK, D), BF16),
            pltpu.VMEM((2, TOK, D), BF16),
            pltpu.VMEM((3, D, 640), BF16),
            pltpu.VMEM((640, D), BF16),
            pltpu.VMEM((1728, D), BF16),
            pltpu.VMEM((D, D), BF16),
            pltpu.VMEM((D, 2 * TOK), F32),
            pltpu.VMEM((HALF, 144, 2 * TOK), BF16),
            pltpu.VMEM((HALF, 144, 2 * TOK), BF16),
            pltpu.VMEM((HALF, 160, 2 * TOK), F32),
            pltpu.VMEM((HALF, 8, 2 * TOK), F32),
            pltpu.VMEM((2, 2, 576, TOK), F32),
            pltpu.VMEM((2, 2, 576, TOK), BF16),
            pltpu.VMEM((2, 576, TOK), BF16),
            dma((4,)),
            dma((5,)),
            dma((4,)),
            dma((2,)),
            dma((1,)),
            dma((12,)),
        ],
        compiler_params=pltpu.CompilerParams(
            collective_id=1, has_side_effects=True, vmem_limit_bytes=60 * 2**20
        ),
        cost_estimate=pl.CostEstimate(flops=43_000_000_000, bytes_accessed=14_000_000, transcendentals=8_400_000),
        name="spatial_block",
    )(z, dz, mod, dmod, wqkv, wout, qg, kg)


def temporal_kernel(
    x_ref, mod_ref, dmod_ref, wqkv_ref, wout_ref, qg_ref, kg_ref, out_ref, h2, win, wt, wout, kt, at, wsem
):
    wcopies = [
        pltpu.make_async_copy(wqkv_ref.at[:, pl.ds(D * j, D)], win.at[j], wsem.at[j]) for j in range(3)
    ] + [pltpu.make_async_copy(wout_ref, wout, wsem.at[3])]
    for copy in wcopies:
        copy.start()

    def rows_of(which):
        return lambda a, n: x_ref[pl.ds(a // 16, n // 16), which].reshape(n, D)

    def put(at_row, rows, h, dh):
        h2[pl.ds(at_row, rows), :] = h
        h2[pl.ds(at_row + TOK, rows), :] = dh

    normed_hidden(rows_of(0), rows_of(1), mod_ref, dmod_ref, put)

    for j in range(3):
        wcopies[j].wait()
        for i in range(9):
            wt[pl.ds(D * j + 128 * i, 128), :] = win[j, :, pl.ds(128 * i, 128)].T

    def project(n, _):
        rows = pl.ds(pl.multiple_of(n * 288, 16), 288)
        kt[rows, :] = dot(wt[rows, :], h2[...], ((1,), (1,)))
        return 0

    lax.fori_loop(0, 12, project, 0)

    ki = lax.broadcasted_iota(jnp.int32, (TOK, TOK), 0)
    qi = lax.broadcasted_iota(jnp.int32, (TOK, TOK), 1)
    same = (ki & 15) == (qi & 15)

    def one_head(h, _):
        def part(j):
            rows = pl.ds(pl.multiple_of(j * D + h * HD, 8), HD)
            return kt[rows, 0:TOK], kt[rows, TOK : 2 * TOK]

        qs, qd = query_operands(*part(0), qg_ref[...])
        kd = key_operand(*part(1), kg_ref[...])
        ve, vg = value_operands(*part(2))
        s = jnp.where(same, dot(kd, qs, ((1,), (0,))), -1e30)
        ds = dot(kd, qd, ((1,), (0,)))
        e = jnp.exp2(s - jnp.max(s, 0, keepdims=True))
        g = e * ds
        ae = dot(ve, e.astype(BF16), ((1,), (0,)))
        ag = dot(vg, g.astype(BF16), ((1,), (0,)))
        inv = 1.0 / ae[144:145]
        attn = ae[0:72] * inv
        rows = pl.ds(pl.multiple_of(h * HD, 8), HD)
        at[0, rows, :] = attn
        at[1, rows, :] = (ae[72:144] + ag[0:72] - ag[73:74] * attn) * inv
        return 0

    lax.fori_loop(0, HEADS, one_head, 0)

    wcopies[3].wait()
    proj = dot(at[0].astype(BF16), wout[...], ((0,), (0,)))
    dproj = dot(at[1].astype(BF16), wout[...], ((0,), (0,)))
    gate = mod_ref[2:3, :]
    dgate = dmod_ref[2:3, :]
    z = x_ref[:, 0].reshape(TOK, D).astype(F32)
    dz = x_ref[:, 1].reshape(TOK, D).astype(F32)
    out_ref[:, 0] = (z + gate * proj).astype(BF16).reshape(16, 16, D)
    out_ref[:, 1] = (dz + gate * dproj + dgate * proj).astype(BF16).reshape(16, 16, D)


def temporal(x, mod, dmod, wqkv, wout, qg, kg):
    vmem = pl.BlockSpec(memory_space=pltpu.VMEM)
    hbm = pl.BlockSpec(memory_space=pl.ANY)
    return pl.pallas_call(
        temporal_kernel,
        out_shape=jax.ShapeDtypeStruct((16, 2, 16, D), BF16),
        in_specs=[vmem, vmem, vmem, hbm, hbm, vmem, vmem],
        out_specs=vmem,
        scratch_shapes=[
            pltpu.VMEM((2 * TOK, D), BF16),
            pltpu.VMEM((3, D, D), BF16),
            pltpu.VMEM((3 * D, D), BF16),
            pltpu.VMEM((D, D), BF16),
            pltpu.VMEM((3 * D, 2 * TOK), F32),
            pltpu.VMEM((2, D, TOK), F32),
            pltpu.SemaphoreType.DMA((4,)),
        ],
        compiler_params=pltpu.CompilerParams(vmem_limit_bytes=60 * 2**20),
        name="temporal_block",
    )(x, mod, dmod, wqkv, wout, qg, kg)


OFFSETS = [(a, b, d) for a in (0, 1) for b in (0, 2, 1, 3) for d in (0, 1)]


def member(zh, y, zl):
    return (zh * 4 + y) * 2 + zl


def forward_kernel(src_ref, out_ref, ss, rs, ls):
    zh, y, c, zl, x = coords()
    me = member(zh, y, zl)
    barrier = pltpu.get_barrier_semaphore()
    copies = []
    keep = pltpu.make_async_copy(src_ref.at[me], out_ref.at[me], ls)
    keep.start()
    for n, (a, b, d) in enumerate(OFFSETS):
        if n == 0:
            continue
        back = (lax.rem(zh + a, 2), lax.rem(y + 4 - b, 4), c, lax.rem(zl + d, 2), x)
        pl.semaphore_signal(barrier, inc=1, device_id=back, device_id_type=MESH)
        to = (lax.rem(zh + a, 2), lax.rem(y + b, 4), c, lax.rem(zl + d, 2), x)
        copies.append(
            pltpu.make_async_remote_copy(
                src_ref=src_ref.at[member(to[0], to[1], to[3])],
                dst_ref=out_ref.at[me],
                send_sem=ss.at[n],
                recv_sem=rs.at[n],
                device_id=to,
                device_id_type=MESH,
            )
        )
    pl.semaphore_wait(barrier, 15)
    for copy in copies:
        copy.start()
    keep.wait()
    for copy in copies:
        copy.wait()


def return_kernel(src_ref, out_ref, dout_ref, got, ss, rs, ls):
    zh, y, c, zl, x = coords()
    me = member(zh, y, zl)
    barrier = pltpu.get_barrier_semaphore()
    copies = []
    rows = pl.ds(pl.multiple_of(16 * me, 16), 16)
    for n, (a, b, d) in enumerate(OFFSETS):
        back = (lax.rem(zh + a, 2), lax.rem(y + 4 - b, 4), zl, lax.rem(c + d, 2), x)
        z2, y2, l2 = lax.rem(zh + a, 2), lax.rem(y + b, 4), lax.rem(zl + d, 2)
        copy = pltpu.make_async_remote_copy(
            src_ref=src_ref.at[member(z2, y2, l2)],
            dst_ref=got.at[:, rows],
            send_sem=ss.at[n],
            recv_sem=rs.at[n],
            device_id=(z2, y2, l2, c, x),
            device_id_type=MESH,
        )
        copies.append(copy)

        def greet(back=back):
            pl.semaphore_signal(barrier, inc=1, device_id=back, device_id_type=MESH)

        if n == 0:
            pl.when(c != zl)(greet)
        else:
            greet()
    keep = pltpu.make_async_copy(src_ref.at[me], got.at[:, rows], ls)

    @pl.when(c == zl)
    def _():
        keep.start()
        pl.semaphore_wait(barrier, 15)

    @pl.when(c != zl)
    def _():
        pl.semaphore_wait(barrier, 16)
        copies[0].start()

    for copy in copies[1:]:
        copy.start()

    @pl.when(c == zl)
    def _():
        keep.wait()

    @pl.when(c != zl)
    def _():
        copies[0].wait()

    for copy in copies[1:]:
        copy.wait()
    out_ref[...] = got[0]
    dout_ref[...] = got[1]


def exchange(x, back):
    vmem = pl.BlockSpec(memory_space=pltpu.VMEM)
    dma = pltpu.SemaphoreType.DMA
    sems = [dma((16,)), dma((16,)), dma]
    one = jax.ShapeDtypeStruct((TOK, D), BF16)
    return pl.pallas_call(
        return_kernel if back else forward_kernel,
        out_shape=(one, one) if back else jax.ShapeDtypeStruct(x.shape, x.dtype),
        in_specs=[vmem],
        out_specs=(vmem, vmem) if back else vmem,
        scratch_shapes=([pltpu.VMEM((2, TOK, D), BF16)] if back else []) + sems,
        compiler_params=pltpu.CompilerParams(
            collective_id=3 if back else 2, has_side_effects=True, vmem_limit_bytes=32 * 2**20
        ),
        name="return_frames" if back else "send_positions",
    )(x)


def body(
    latent,
    latent_tangent,
    modulation,
    modulation_tangent,
    w_qkv_s,
    w_out_s,
    q_gain_s,
    k_gain_s,
    w_qkv_t,
    w_out_t,
    q_gain_t,
    k_gain_t,
):
    shape = latent.shape
    column = lambda gain: gain.reshape(HD, 1)
    x = spatial(
        latent.reshape(TOK, D), latent_tangent.reshape(TOK, D), modulation, modulation_tangent,
        w_qkv_s, w_out_s, column(q_gain_s), column(k_gain_s),
    )
    x = exchange(x, False)
    x = temporal(x, modulation, modulation_tangent, w_qkv_t, w_out_t, column(q_gain_t), column(k_gain_t))
    out, dout = exchange(x, True)
    return out.reshape(shape), dout.reshape(shape)


def solution(mesh):
    split = Mesh(mesh.devices.reshape(2, 4, 2, 2, 4), AXES)
    tokens = P(("zh", "y", "core"), ("zl", "x"), None, None)
    return jax.shard_map(
        body, mesh=split, in_specs=(tokens, tokens) + (P(),) * 10, out_specs=(tokens, tokens), check_vma=False
    )
```

```python
import functools
import math

import jax
import jax.numpy as jnp
from jax import lax
from jax.experimental import pallas as pl
from jax.experimental.pallas import tpu as pltpu
from jax.sharding import Mesh, PartitionSpec as P

D = 1152
HEADS = 16
HD = 72
EPS = 1e-06
AXES = ("zh", "y", "core", "zl", "x")
TOK = 256
HALF = 8
FACTOR = 1.0 / math.sqrt(HD)
LOG2E = 1.4426950408889634
MESH = pl.DeviceIdType.MESH
F32 = jnp.float32
BF16 = jnp.bfloat16


def coords():
    return tuple(lax.axis_index(a) for a in AXES)


def dot(a, b, dims):
    return lax.dot_general(a, b, (dims, ((), ())), preferred_element_type=F32)


def normed_hidden(count, z_of, dz_of, mod_ref, dmod_ref, put):
    rows = 32

    def step(i, _):
        at = pl.multiple_of(i * rows, rows)
        z = z_of(at, rows).astype(F32)
        dz = dz_of(at, rows).astype(F32)
        cent = z - jnp.mean(z, -1, keepdims=True)
        rstd = lax.rsqrt(jnp.mean(cent * cent, -1, keepdims=True) + EPS)
        normed = cent * rstd
        dcent = dz - jnp.mean(dz, -1, keepdims=True)
        dnormed = rstd * (dcent - normed * jnp.mean(normed * dcent, -1, keepdims=True))
        scale = 1.0 + mod_ref[1:2, :]
        hidden = normed * scale + mod_ref[0:1, :]
        dhidden = dnormed * scale + normed * dmod_ref[1:2, :] + dmod_ref[0:1, :]
        put(at, rows, hidden.astype(BF16), dhidden.astype(BF16))
        return 0

    lax.fori_loop(0, count // rows, step, 0)


def head_norm(u, du):
    r = lax.rsqrt(jnp.mean(u * u, 0, keepdims=True) + EPS)
    unit = u * r
    return unit, r * (du - unit * jnp.mean(unit * du, 0, keepdims=True))


def query_operands(q, dq, gain):
    unit, inner = head_norm(q, dq)
    qn = unit * (gain * FACTOR)
    dqn = inner * (gain * FACTOR)
    first = jnp.concatenate([qn * LOG2E, jnp.zeros_like(qn)], 0).astype(BF16)
    second = jnp.concatenate([dqn, qn], 0).astype(BF16)
    return first, second


def key_operand(k, dk, gain):
    unit, inner = head_norm(k, dk)
    both = jnp.concatenate([unit * gain, inner * gain], 0)
    return both.T.astype(BF16)


def value_operands(v, dv):
    n = v.shape[1]
    row16 = lax.broadcasted_iota(jnp.int32, (16, n), 0)
    row8 = lax.broadcasted_iota(jnp.int32, (8, n), 0)
    for_e = jnp.concatenate([v, dv, (row16 == 0).astype(F32)], 0).astype(BF16)
    for_g = jnp.concatenate([v, (row8 == 1).astype(F32)], 0).astype(BF16)
    return for_e, for_g


def normalised(acc):
    inv = 1.0 / acc[144:145]
    attn = acc[0:72] * inv
    dattn = (acc[72:144] - acc[145:146] * attn) * inv
    return attn, dattn


OFFSETS = [(a, b, d) for a in (0, 1) for b in (2, 0, 1, 3) for d in (1, 0)]
SELF = OFFSETS.index((0, 0, 0))
CHUNK = 128


def member(zh, y, zl):
    return (zh * 4 + y) * 2 + zl


def both_halves(x):
    n = x.shape[0] * 8
    return x[:, 0:8].reshape(n, D), x[:, 8:16].reshape(n, D)


def joined(z, dz):
    n = z.shape[0] // 8
    return jnp.concatenate([z.reshape(n, 8, D), dz.reshape(n, 8, D)], 1).astype(BF16)


def block_kernel(
    z_ref, dz_ref, mod_ref, dmod_ref, wqkv_s, wout_s, qg_s, kg_s, wqkv_t, wout_t, qg_t, kg_t,
    out_ref, dout_ref,
    hb, zb, stage, wtmp, wt, wos, wtt, wot, kt, qs, qd, kds, ves, vgs, acc, mx, at, mine, theirs,
    th, tx, rx, ty, got, gains,
    stage_sem, wsem, ro, rb, rz, rx_sem, ss, sw_s, sw_r, fs, fr, fl, gs, gr, gl,
):
    zh, y, c, zl, x = coords()
    right = (zh, y, c, zl, lax.rem(x + 1, 4))
    left = (zh, y, c, zl, lax.rem(x + 3, 4))
    sib = (zh, y, 1 - c, zl, x)
    partner = (zh, y, zl, c, x)
    t = lax.rem(c + zl, 2)
    me = member(zh, y, zl)
    same = t == 0
    moved = t == 1

    barrier = pltpu.get_barrier_semaphore()

    def greet(peer):
        pl.semaphore_signal(barrier, inc=1, device_id=peer, device_id_type=MESH)

    for peer in (right, left, sib):
        greet(peer)
    pl.when(moved)(lambda: greet(partner))
    for n, (a, b, d) in enumerate(OFFSETS):
        zh2, y2 = lax.rem(zh + a, 2), lax.rem(y + 4 - b, 4)
        back = (zh2, y2, zl, lax.rem(c + d, 2), x)
        if n == SELF:
            pl.when(moved)(functools.partial(greet, back))
        else:
            greet((zh2, y2, c, lax.rem(zl + d, 2), x))
            greet(back)

    out_w = [pltpu.make_async_copy(wout_s, wos, wsem.at[0]), pltpu.make_async_copy(wout_t, wot, wsem.at[1])]

    def window(j):
        cols = pl.ds(pl.multiple_of(D * j + 512 * c, 128), 640)
        return pltpu.make_async_copy(wqkv_s.at[:, cols], stage.at[j % 2], stage_sem.at[j % 2])

    def piece(i, slot):
        cols = pl.ds(pl.multiple_of(384 * i, 128), 384)
        return pltpu.make_async_copy(wqkv_t.at[:, cols], stage.at[slot, :, pl.ds(0, 384)], stage_sem.at[slot])

    window(0).start()
    window(1).start()
    for copy in out_w:
        copy.start()

    def remote(src, dst, send, recv, to):
        return pltpu.make_async_remote_copy(
            src_ref=src, dst_ref=dst, send_sem=send, recv_sem=recv, device_id=to, device_id_type=MESH
        )

    def slot(dx):
        return hb.at[2 * dx + t]

    to_right = remote(slot(0), slot(3), ss.at[0], ro.at[3], right)
    to_left = remote(slot(0), slot(1), ss.at[1], ro.at[1], left)
    to_sib = [remote(slot(dx), slot(dx), ss.at[2 + dx], rb.at[dx], sib) for dx in range(4)]
    on_left = remote(slot(1).at[0], slot(2).at[0], ss.at[6], ro.at[2], left)
    on_right = remote(slot(3).at[1], slot(2).at[1], ss.at[7], ro.at[4], right)
    swaps = [
        remote(hb.at[8, :, pl.ds(64 * q, 64)], hb.at[1, :, pl.ds(64 * q, 64)], sw_s.at[q], sw_r.at[q], partner)
        for q in range(4)
    ]
    swap_z = remote(z_ref, zb.at[0], ss.at[8], rz.at[0], partner)
    swap_dz = remote(dz_ref, zb.at[1], ss.at[9], rz.at[1], partner)

    own = 8 * t
    for q in range(4):

        def put(at_row, rows, h, dh):
            hb[own, 0, pl.ds(64 * q + at_row, rows), :] = h
            hb[own, 1, pl.ds(64 * q + at_row, rows), :] = dh

        normed_hidden(
            64,
            lambda a, n: z_ref[pl.ds(64 * q + a, n), :],
            lambda a, n: dz_ref[pl.ds(64 * q + a, n), :],
            mod_ref, dmod_ref, put,
        )
        if q == 0:
            pl.when(same)(lambda: pl.semaphore_wait(barrier, 33))
            pl.when(moved)(lambda: pl.semaphore_wait(barrier, 35))
        pl.when(moved)(swaps[q].start)

    @pl.when(same)
    def _():
        to_sib[0].start()
        to_right.start()
        to_left.start()
        zb[0] = z_ref[...]
        zb[1] = dz_ref[...]

    for j in range(3):
        window(j).wait()
        for i in range(5):
            wtmp[pl.ds(128 * i, 128), :] = stage[j % 2, :, pl.ds(128 * i, 128)].T
        if j == 0:
            window(2).start()
        else:
            piece(j - 1, j % 2).start()
        wt[pl.ds(576 * j, 576), :] = wtmp[pl.ds(pl.multiple_of(64 * c, 64), 576), :]

    for i, g in enumerate((qg_s, kg_s, qg_t, kg_t)):
        rows = lax.broadcasted_iota(jnp.int32, (HD, HD), 0)
        cols = lax.broadcasted_iota(jnp.int32, (HD, HD), 1)
        gains[i] = jnp.sum(jnp.where(rows == cols, g[...], 0.0), 1, keepdims=True)

    acc[...] = jnp.zeros_like(acc)
    mx[...] = jnp.full_like(mx, -1e30)

    def turn_piece(i, _):
        which = lax.rem(i + 1, 2)
        piece(i, which).wait()
        for n in range(3):
            rows = pl.ds(pl.multiple_of(384 * i + 128 * n, 128), 128)
            wtt[rows, :] = stage[which, :, pl.ds(128 * n, 128)].T

        @pl.when(i < 7)
        def _():
            piece(i + 2, which).start()

        return 0

    lax.fori_loop(0, 9, turn_piece, 0)

    @pl.when(moved)
    def _():
        for copy in swaps:
            copy.wait_recv()
        to_sib[0].start()
        to_right.start()
        to_left.start()
        swap_z.start()
        swap_dz.start()

    to_sib[0].wait_recv()

    for part in range(2):
        kt[0:576, 512 * part : 512 * part + 512] = dot(wt[0:576, :], hb[part].reshape(2 * TOK, D), ((1,), (1,)))

    def make_query(h, _):
        rows = pl.ds(pl.multiple_of(h * HD, 8), HD)
        for part in range(2):
            o = 512 * part
            first, second = query_operands(kt[rows, o : o + 256], kt[rows, o + 256 : o + 512], gains[0])
            qs[h, :, 256 * part : 256 * part + 256] = first
            qd[h, :, 256 * part : 256 * part + 256] = second
        return 0

    lax.fori_loop(0, HALF, make_query, 0, unroll=2)

    def two_shards(i, _):
        for n in (0, 1):

            @pl.when((i == 1 + n) & (t == n))
            def _():
                to_left.wait_recv()
                on_left.start()
                to_sib[1].start()
                to_right.wait_recv()
                on_right.start()
                to_sib[3].start()

            @pl.when((i == 1 + n) & (t != n))
            def _():
                to_sib[1].wait_recv()
                to_sib[3].wait_recv()

        @pl.when(i == 3)
        def _():
            on_left.wait_recv()
            on_right.wait_recv()
            to_sib[2].start()
            to_sib[2].wait_recv()

        first = jnp.where(i == 0, 0, i + 1)
        second = jnp.where(i == 0, 1, jnp.where(i == 3, 5, i + 5))
        for s, index in enumerate((first, second)):
            kt[:, 512 * s : 512 * s + 512] = dot(wt[576:1728, :], hb[index].reshape(2 * TOK, D), ((1,), (1,)))

        def one_head(h, _):
            krow = pl.ds(pl.multiple_of(h * HD, 8), HD)
            vrow = pl.ds(pl.multiple_of(576 + h * HD, 8), HD)
            for s in range(2):
                o = 512 * s
                keys = slice(256 * s, 256 * s + 256)
                kds[h, keys, :] = key_operand(kt[krow, o : o + 256], kt[krow, o + 256 : o + 512], gains[1])
                ve, vg = value_operands(kt[vrow, o : o + 256], kt[vrow, o + 256 : o + 512])
                ves[h, :, keys] = ve
                vgs[h, :, keys] = vg
            kd = kds[h]
            s = dot(kd, qs[h], ((1,), (0,)))
            ds = dot(kd, qd[h], ((1,), (0,)))
            old = mx[h, 0:1, :]
            new = jnp.maximum(old, jnp.max(s, 0, keepdims=True))
            mx[h, 0:1, :] = new
            e = jnp.exp2(s - new)
            g = e * ds
            keep = jnp.exp2(old - new)
            of_e = dot(ves[h], e.astype(BF16), ((1,), (0,)))
            of_g = dot(vgs[h], g.astype(BF16), ((1,), (0,)))
            acc[h, 0:72, :] = acc[h, 0:72, :] * keep + of_e[0:72]
            acc[h, 72:152, :] = acc[h, 72:152, :] * keep + of_e[72:152] + of_g
            return 0

        lax.fori_loop(0, HALF, one_head, 0, unroll=8)
        return 0

    lax.fori_loop(0, 4, two_shards, 0)

    def finish_head(h, _):
        attn, dattn = normalised(acc[h])
        rows = pl.ds(pl.multiple_of(h * HD, 8), HD)
        for part in range(2):
            for q in range(2):
                cols = slice(256 * part + 128 * q, 256 * part + 128 * q + 128)
                at[part, q, rows, 0:128] = attn[:, cols]
                at[part, q, rows, 128:256] = dattn[:, cols]
        return 0

    lax.fori_loop(0, HALF, finish_head, 0, unroll=2)
    mine[1] = at[1 - t].astype(BF16)
    trade = remote(mine.at[1], theirs, ss.at[10], rx_sem.at[0], sib)
    trade.start()
    mine[0] = at[t].astype(BF16)
    out_w[0].wait()
    out_w[1].wait()

    @pl.when(moved)
    def _():
        swap_z.wait_recv()
        swap_dz.wait_recv()

    trade.wait_recv()

    def forward(q, n):
        a, b, d = OFFSETS[n]
        to = (lax.rem(zh + a, 2), lax.rem(y + b, 4), c, lax.rem(zl + d, 2), x)
        return remote(
            tx.at[q, member(to[0], to[1], to[3])], rx.at[q, me], fs.at[16 * q + n], fr.at[16 * q + n], to
        )

    def forward_own(q):
        return pltpu.make_async_copy(tx.at[q, me], rx.at[q, me], fl.at[q])

    def give_back(q, n):
        a, b, d = OFFSETS[n]
        z2, y2, l2 = lax.rem(zh + a, 2), lax.rem(y + b, 4), lax.rem(zl + d, 2)
        return remote(
            ty.at[q, member(z2, y2, l2)], got.at[q, me], gs.at[16 * q + n], gr.at[16 * q + n], (z2, y2, l2, c, x)
        )

    def give_own(q):
        return pltpu.make_async_copy(ty.at[q, me], got.at[q, me], gl.at[q])

    others = [n for n in range(16) if n != SELF]
    gate = mod_ref[2:3, :]
    dgate = dmod_ref[2:3, :]
    lo = pl.ds(pl.multiple_of(576 * c, 16), 576)
    hi = pl.ds(pl.multiple_of(576 * (1 - c), 16), 576)

    def spatial_out(q, _):
        both = dot(mine[0, q], wos[lo, :], ((0,), (0,))) + dot(theirs[q], wos[hi, :], ((0,), (0,)))
        rows = pl.ds(pl.multiple_of(CHUNK * q, CHUNK), CHUNK)
        proj, dproj = both[0:CHUNK], both[CHUNK:]
        tx[q] = joined(
            zb[0, rows, :].astype(F32) + gate * proj,
            zb[1, rows, :].astype(F32) + gate * dproj + dgate * proj,
        )
        forward_own(q).start()
        for n in others:
            forward(q, n).start()
        return 0

    lax.fori_loop(0, 2, spatial_out, 0)

    ki = lax.broadcasted_iota(jnp.int32, (CHUNK, CHUNK), 0)
    qi = lax.broadcasted_iota(jnp.int32, (CHUNK, CHUNK), 1)
    place = (ki & 7) == (qi & 7)

    def temporal_chunk(q, _):
        forward_own(q).wait()
        for n in others:
            forward(q, n).wait_recv()

        def put(at_row, rows, h, dh):
            th[pl.ds(at_row, rows), :] = h
            th[pl.ds(CHUNK + at_row, rows), :] = dh

        def half(which):
            return lambda a, n: both_halves(rx[q, pl.ds(a // 8, n // 8)].astype(F32))[which]

        normed_hidden(CHUNK, half(0), half(1), mod_ref, dmod_ref, put)
        for j in range(3):
            kt[:, 256 * j : 256 * j + 256] = dot(wtt[D * j : D * j + D, :], th[...], ((1,), (1,)))

        def one_head(h, _):
            rows = pl.ds(pl.multiple_of(h * HD, 8), HD)
            first, second = query_operands(kt[rows, 0:128], kt[rows, 128:256], gains[2])
            kd = key_operand(kt[rows, 256:384], kt[rows, 384:512], gains[3])
            ve, vg = value_operands(kt[rows, 512:640], kt[rows, 640:768])
            both = dot(kd, jnp.concatenate([first, second], 1), ((1,), (0,)))
            s = jnp.where(place, both[:, 0:128], -1e30)
            e = jnp.exp2(s - jnp.max(s, 0, keepdims=True))
            g = e * both[:, 128:256]
            of_e = dot(ve, e.astype(BF16), ((1,), (0,)))
            of_g = dot(vg, g.astype(BF16), ((1,), (0,)))
            inv = 1.0 / of_e[144:145]
            attn = of_e[0:72] * inv
            dattn = (of_e[72:144] + of_g[0:72] - of_g[73:74] * attn) * inv
            to_rows = pl.ds(pl.multiple_of(lax.rem(h, 8) * HD, 8), HD)
            at[0, h // 8, to_rows, 0:128] = attn
            at[0, h // 8, to_rows, 128:256] = dattn
            return 0

        lax.fori_loop(0, HEADS, one_head, 0, unroll=4)
        both = dot(at[0, 0].astype(BF16), wot[0:576, :], ((0,), (0,)))
        both += dot(at[0, 1].astype(BF16), wot[576:1152, :], ((0,), (0,)))
        proj, dproj = both[0:CHUNK], both[CHUNK:]
        z, dz = both_halves(rx[q].astype(F32))
        ty[q] = joined(z + gate * proj, dz + gate * dproj + dgate * proj)
        pl.when(same)(lambda: give_own(q).start())
        pl.when(moved)(lambda: give_back(q, SELF).start())
        for n in others:
            give_back(q, n).start()
        return 0

    lax.fori_loop(0, 2, temporal_chunk, 0)

    def collect(q, _):
        pl.when(same)(lambda: give_own(q).wait())
        pl.when(moved)(lambda: give_back(q, SELF).wait())
        for n in others:
            give_back(q, n).wait()
            forward(q, n).wait_send()
        rows = pl.ds(pl.multiple_of(CHUNK * q, CHUNK), CHUNK)
        z, dz = both_halves(got[q].astype(F32))
        out_ref[rows, :] = z.astype(BF16)
        dout_ref[rows, :] = dz.astype(BF16)
        return 0

    lax.fori_loop(0, 2, collect, 0)

    for copy in (to_right, to_left, *to_sib, on_left, on_right, trade):
        copy.wait_send()

    @pl.when(moved)
    def _():
        for copy in (*swaps, swap_z, swap_dz):
            copy.wait_send()


def body(
    latent,
    latent_tangent,
    modulation,
    modulation_tangent,
    w_qkv_s,
    w_out_s,
    q_gain_s,
    k_gain_s,
    w_qkv_t,
    w_out_t,
    q_gain_t,
    k_gain_t,
):
    shape = latent.shape
    vmem = pl.BlockSpec(memory_space=pltpu.VMEM)
    hbm = pl.BlockSpec(memory_space=pl.ANY)
    dma = pltpu.SemaphoreType.DMA
    one = jax.ShapeDtypeStruct((TOK, D), BF16)
    row = lambda gain: gain.reshape(1, HD)
    out, dout = pl.pallas_call(
        block_kernel,
        out_shape=(one, one),
        in_specs=[vmem, vmem, vmem, vmem, hbm, hbm, vmem, vmem, hbm, hbm, vmem, vmem],
        out_specs=(vmem, vmem),
        scratch_shapes=[
            pltpu.VMEM((9, 2, TOK, D), BF16),
            pltpu.VMEM((2, TOK, D), BF16),
            pltpu.VMEM((2, D, 640), BF16),
            pltpu.VMEM((640, D), BF16),
            pltpu.VMEM((1728, D), BF16),
            pltpu.VMEM((D, D), BF16),
            pltpu.VMEM((3 * D, D), BF16),
            pltpu.VMEM((D, D), BF16),
            pltpu.VMEM((D, 4 * TOK), F32),
            pltpu.VMEM((HALF, 144, 2 * TOK), BF16),
            pltpu.VMEM((HALF, 144, 2 * TOK), BF16),
            pltpu.VMEM((HALF, 2 * TOK, 144), BF16),
            pltpu.VMEM((HALF, 160, 2 * TOK), BF16),
            pltpu.VMEM((HALF, 80, 2 * TOK), BF16),
            pltpu.VMEM((HALF, 160, 2 * TOK), F32),
            pltpu.VMEM((HALF, 8, 2 * TOK), F32),
            pltpu.VMEM((2, 2, 576, TOK), F32),
            pltpu.VMEM((2, 2, 576, TOK), BF16),
            pltpu.VMEM((2, 576, TOK), BF16),
            pltpu.VMEM((TOK, D), BF16),
            pltpu.VMEM((2, 16, 16, D), BF16),
            pltpu.VMEM((2, 16, 16, D), BF16),
            pltpu.VMEM((2, 16, 16, D), BF16),
            pltpu.VMEM((2, 16, 16, D), BF16),
            pltpu.VMEM((4, HD, 1), F32),
            dma((2,)), dma((2,)), dma((5,)), dma((4,)), dma((2,)), dma((1,)), dma((11,)),
            dma((4,)), dma((4,)),
            dma((32,)), dma((32,)), dma((2,)), dma((32,)), dma((32,)), dma((2,)),
        ],
        compiler_params=pltpu.CompilerParams(
            collective_id=1, has_side_effects=True, vmem_limit_bytes=63 * 2**20
        ),
        cost_estimate=pl.CostEstimate(flops=53_000_000_000, bytes_accessed=25_000_000, transcendentals=9_000_000),
        name="blocks",
    )(
        latent.reshape(TOK, D), latent_tangent.reshape(TOK, D), modulation, modulation_tangent,
        w_qkv_s, w_out_s, row(q_gain_s), row(k_gain_s), w_qkv_t, w_out_t, row(q_gain_t), row(k_gain_t),
    )
    return out.reshape(shape), dout.reshape(shape)


def solution(mesh):
    split = Mesh(mesh.devices.reshape(2, 4, 2, 2, 4), AXES)
    tokens = P(("zh", "y", "core"), ("zl", "x"), None, None)
    return jax.shard_map(
        body, mesh=split, in_specs=(tokens, tokens) + (P(),) * 10, out_specs=(tokens, tokens), check_vma=False
    )
```

```python
import functools
import math

import jax
import jax.numpy as jnp
from jax import lax
from jax.experimental import pallas as pl
from jax.experimental.pallas import tpu as pltpu
from jax.sharding import Mesh, PartitionSpec as P

D = 1152
HEADS = 16
HD = 72
EPS = 1e-06
AXES = ("zh", "y", "core", "zl", "x")
TOK = 256
HALF = 8
FACTOR = 1.0 / math.sqrt(HD)
LOG2E = 1.4426950408889634
MESH = pl.DeviceIdType.MESH
F32 = jnp.float32
BF16 = jnp.bfloat16


def coords():
    return tuple(lax.axis_index(a) for a in AXES)


def dot(a, b, dims):
    return lax.dot_general(a, b, (dims, ((), ())), preferred_element_type=F32)


def normed_hidden(count, z_of, dz_of, mod_ref, dmod_ref, put):
    rows = 32

    def step(i, _):
        at = pl.multiple_of(i * rows, rows)
        z = z_of(at, rows).astype(F32)
        dz = dz_of(at, rows).astype(F32)
        cent = z - jnp.mean(z, -1, keepdims=True)
        rstd = lax.rsqrt(jnp.mean(cent * cent, -1, keepdims=True) + EPS)
        normed = cent * rstd
        dcent = dz - jnp.mean(dz, -1, keepdims=True)
        dnormed = rstd * (dcent - normed * jnp.mean(normed * dcent, -1, keepdims=True))
        scale = 1.0 + mod_ref[1:2, :]
        hidden = normed * scale + mod_ref[0:1, :]
        dhidden = dnormed * scale + normed * dmod_ref[1:2, :] + dmod_ref[0:1, :]
        put(at, rows, hidden.astype(BF16), dhidden.astype(BF16))
        return 0

    lax.fori_loop(0, count // rows, step, 0)


def head_norm(u, du):
    r = lax.rsqrt(jnp.mean(u * u, 0, keepdims=True) + EPS)
    unit = u * r
    return unit, r * (du - unit * jnp.mean(unit * du, 0, keepdims=True))


def query_operands(q, dq, gain):
    unit, inner = head_norm(q, dq)
    qn = unit * (gain * FACTOR)
    dqn = inner * (gain * FACTOR)
    first = jnp.concatenate([qn * LOG2E, jnp.zeros_like(qn)], 0).astype(BF16)
    second = jnp.concatenate([dqn, qn], 0).astype(BF16)
    return first, second


def key_operand(k, dk, gain):
    unit, inner = head_norm(k, dk)
    both = jnp.concatenate([unit * gain, inner * gain], 0)
    return both.T.astype(BF16)


def value_operands(v, dv):
    n = v.shape[1]
    row16 = lax.broadcasted_iota(jnp.int32, (16, n), 0)
    row8 = lax.broadcasted_iota(jnp.int32, (8, n), 0)
    for_e = jnp.concatenate([v, dv, (row16 == 0).astype(F32)], 0).astype(BF16)
    for_g = jnp.concatenate([v, (row8 == 1).astype(F32)], 0).astype(BF16)
    return for_e, for_g


def normalised(acc):
    inv = 1.0 / acc[144:145]
    attn = acc[0:72] * inv
    dattn = (acc[72:144] - acc[145:146] * attn) * inv
    return attn, dattn


OFFSETS = [(a, b, d) for a in (0, 1) for b in (2, 0, 1, 3) for d in (1, 0)]
SELF = OFFSETS.index((0, 0, 0))
CHUNK = 128


def member(zh, y, zl):
    return (zh * 4 + y) * 2 + zl


def both_halves(x):
    n = x.shape[0] * 8
    return x[:, 0:8].reshape(n, D), x[:, 8:16].reshape(n, D)


def joined(z, dz):
    n = z.shape[0] // 8
    return jnp.concatenate([z.reshape(n, 8, D), dz.reshape(n, 8, D)], 1).astype(BF16)


def block_kernel(
    z_ref, dz_ref, mod_ref, dmod_ref, wqkv_s, wout_s, qg_s, kg_s, wqkv_t, wout_t, qg_t, kg_t,
    out_ref,
    hb, zb, stage, wtmp, wt, wos, wtt, wot, kt, qs, qd, kds, ves, vgs, acc, mx, at, mine, theirs,
    th, tx, rx, ty, got, gains,
    relay, stage_sem, wsem, ro, rb, rz, rx_sem, ss, sw_s, sw_r, fs, fr, fl, gs, gr, gl,
):
    zh, y, c, zl, x = coords()
    right = (zh, y, c, zl, lax.rem(x + 1, 4))
    left = (zh, y, c, zl, lax.rem(x + 3, 4))
    sib = (zh, y, 1 - c, zl, x)
    partner = (zh, y, zl, c, x)
    t = lax.rem(c + zl, 2)
    me = member(zh, y, zl)
    same = t == 0
    moved = t == 1

    barrier = pltpu.get_barrier_semaphore()

    def greet(peer):
        pl.semaphore_signal(barrier, inc=1, device_id=peer, device_id_type=MESH)

    z = 2 * zh + zl

    def at_z(n):
        zz = lax.rem(z + n, 4)
        return (zz // 2, y, c, lax.rem(zz, 2), x)

    plane = [(zh, lax.rem(y + n, 4), c, zl, x) for n in (1, 3)] + [at_z(1), at_z(3)]
    for peer in (right, left, sib, *plane):
        greet(peer)
    pl.when(moved)(lambda: greet(partner))

    def tell(n):
        for peer in plane:
            pl.semaphore_signal(relay.at[n], inc=1, device_id=peer, device_id_type=MESH)

    def hear(n):
        pl.semaphore_wait(relay.at[n], 4)

    out_w = [pltpu.make_async_copy(wout_s, wos, wsem.at[0]), pltpu.make_async_copy(wout_t, wot, wsem.at[1])]

    def window(j):
        cols = pl.ds(pl.multiple_of(D * j + 512 * c, 128), 640)
        return pltpu.make_async_copy(wqkv_s.at[:, cols], stage.at[j % 2], stage_sem.at[j % 2])

    def piece(i, slot):
        cols = pl.ds(pl.multiple_of(384 * i, 128), 384)
        return pltpu.make_async_copy(wqkv_t.at[:, cols], stage.at[slot, :, pl.ds(0, 384)], stage_sem.at[slot])

    window(0).start()
    window(1).start()
    for copy in out_w:
        copy.start()

    def remote(src, dst, send, recv, to):
        return pltpu.make_async_remote_copy(
            src_ref=src, dst_ref=dst, send_sem=send, recv_sem=recv, device_id=to, device_id_type=MESH
        )

    def slot(dx):
        return hb.at[2 * dx + t]

    to_right = remote(slot(0), slot(3), ss.at[0], ro.at[3], right)
    to_left = remote(slot(0), slot(1), ss.at[1], ro.at[1], left)
    to_sib = [remote(slot(dx), slot(dx), ss.at[2 + dx], rb.at[dx], sib) for dx in range(4)]
    on_left = remote(slot(1).at[0], slot(2).at[0], ss.at[6], ro.at[2], left)
    on_right = remote(slot(3).at[1], slot(2).at[1], ss.at[7], ro.at[4], right)
    swaps = [
        remote(hb.at[8, :, pl.ds(64 * q, 64)], hb.at[1, :, pl.ds(64 * q, 64)], sw_s.at[q], sw_r.at[q], partner)
        for q in range(4)
    ]
    swap_z = remote(z_ref, zb.at[0], ss.at[8], rz.at[0], partner)
    swap_dz = remote(dz_ref, zb.at[1], ss.at[9], rz.at[1], partner)

    own = 8 * t
    for q in range(4):

        def put(at_row, rows, h, dh):
            hb[own, 0, pl.ds(64 * q + at_row, rows), :] = h
            hb[own, 1, pl.ds(64 * q + at_row, rows), :] = dh

        normed_hidden(
            64,
            lambda a, n: z_ref[pl.ds(64 * q + a, n), :],
            lambda a, n: dz_ref[pl.ds(64 * q + a, n), :],
            mod_ref, dmod_ref, put,
        )
        if q == 0:
            pl.when(same)(lambda: pl.semaphore_wait(barrier, 7))
            pl.when(moved)(lambda: pl.semaphore_wait(barrier, 8))
        pl.when(moved)(swaps[q].start)

    @pl.when(same)
    def _():
        to_sib[0].start()
        to_right.start()
        to_left.start()
        zb[0] = z_ref[...]
        zb[1] = dz_ref[...]

    tell(0)

    for j in range(3):
        window(j).wait()
        for i in range(5):
            wtmp[pl.ds(128 * i, 128), :] = stage[j % 2, :, pl.ds(128 * i, 128)].T
        if j == 0:
            window(2).start()
        else:
            piece(j - 1, j % 2).start()
        wt[pl.ds(576 * j, 576), :] = wtmp[pl.ds(pl.multiple_of(64 * c, 64), 576), :]

    hear(0)
    tell(1)

    for i, g in enumerate((qg_s, kg_s, qg_t, kg_t)):
        rows = lax.broadcasted_iota(jnp.int32, (HD, HD), 0)
        cols = lax.broadcasted_iota(jnp.int32, (HD, HD), 1)
        gains[i] = jnp.sum(jnp.where(rows == cols, g[...], 0.0), 1, keepdims=True)

    acc[...] = jnp.zeros_like(acc)
    mx[...] = jnp.full_like(mx, -1e30)

    def turn_piece(i, _):
        which = lax.rem(i + 1, 2)
        piece(i, which).wait()
        for n in range(3):
            rows = pl.ds(pl.multiple_of(384 * i + 128 * n, 128), 128)
            wtt[rows, :] = stage[which, :, pl.ds(128 * n, 128)].T

        @pl.when(i < 7)
        def _():
            piece(i + 2, which).start()

        return 0

    lax.fori_loop(0, 9, turn_piece, 0)
    hear(1)
    tell(2)

    def query_rows(part):
        kt[0:576, 0:512] = dot(wt[0:576, :], hb[part].reshape(2 * TOK, D), ((1,), (1,)))

        def make_query(h, _):
            rows = pl.ds(pl.multiple_of(h * HD, 8), HD)
            first, second = query_operands(kt[rows, 0:256], kt[rows, 256:512], gains[0])
            qs[h, :, 256 * part : 256 * part + 256] = first
            qd[h, :, 256 * part : 256 * part + 256] = second
            return 0

        lax.fori_loop(0, HALF, make_query, 0, unroll=4)

    pl.when(moved)(to_sib[0].wait_recv)
    query_rows(0)

    @pl.when(moved)
    def _():
        for copy in swaps:
            copy.wait_recv()
        to_sib[0].start()
        to_right.start()
        to_left.start()
        swap_z.start()
        swap_dz.start()

    @pl.when(same)
    def _():
        to_left.wait_recv()
        on_left.start()
        to_sib[1].start()
        to_right.wait_recv()
        on_right.start()
        to_sib[3].start()
        to_sib[0].wait_recv()

    query_rows(1)
    hear(2)
    pl.semaphore_signal(relay.at[3], inc=1, device_id=sib, device_id_type=MESH)

    def two_shards(i, _):
        @pl.when((i == 1) & moved)
        def _():
            to_sib[1].wait_recv()
            to_sib[3].wait_recv()

        @pl.when((i == 2) & moved)
        def _():
            to_left.wait_recv()
            on_left.start()
            to_sib[1].start()
            to_right.wait_recv()
            on_right.start()
            to_sib[3].start()

        @pl.when((i == 2) & same)
        def _():
            to_sib[1].wait_recv()
            to_sib[3].wait_recv()

        @pl.when(i == 3)
        def _():
            on_left.wait_recv()
            on_right.wait_recv()
            to_sib[2].start()
            to_sib[2].wait_recv()

        first = jnp.where(i == 0, 0, i + 1)
        second = jnp.where(i == 0, 1, jnp.where(i == 3, 5, i + 5))
        for s, index in enumerate((first, second)):
            kt[:, 512 * s : 512 * s + 512] = dot(wt[576:1728, :], hb[index].reshape(2 * TOK, D), ((1,), (1,)))

        def one_head(h, _):
            krow = pl.ds(pl.multiple_of(h * HD, 8), HD)
            vrow = pl.ds(pl.multiple_of(576 + h * HD, 8), HD)
            for s in range(2):
                o = 512 * s
                keys = slice(256 * s, 256 * s + 256)
                kds[h, keys, :] = key_operand(kt[krow, o : o + 256], kt[krow, o + 256 : o + 512], gains[1])
                ve, vg = value_operands(kt[vrow, o : o + 256], kt[vrow, o + 256 : o + 512])
                ves[h, :, keys] = ve
                vgs[h, :, keys] = vg
            kd = kds[h]
            s = dot(kd, qs[h], ((1,), (0,)))
            ds = dot(kd, qd[h], ((1,), (0,)))
            old = mx[h, 0:1, :]
            new = jnp.maximum(old, jnp.max(s, 0, keepdims=True))
            mx[h, 0:1, :] = new
            e = jnp.exp2(s - new)
            g = e * ds
            keep = jnp.exp2(old - new)
            of_e = dot(ves[h], e.astype(BF16), ((1,), (0,)))
            of_g = dot(vgs[h], g.astype(BF16), ((1,), (0,)))
            acc[h, 0:72, :] = acc[h, 0:72, :] * keep + of_e[0:72]
            acc[h, 72:152, :] = acc[h, 72:152, :] * keep + of_e[72:152] + of_g
            return 0

        lax.fori_loop(0, HALF, one_head, 0, unroll=8)
        return 0

    lax.fori_loop(0, 4, two_shards, 0)

    def finish_head(h, _):
        attn, dattn = normalised(acc[h])
        rows = pl.ds(pl.multiple_of(h * HD, 8), HD)
        for part in range(2):
            for q in range(2):
                cols = slice(256 * part + 128 * q, 256 * part + 128 * q + 128)
                at[part, q, rows, 0:128] = attn[:, cols]
                at[part, q, rows, 128:256] = dattn[:, cols]
        return 0

    lax.fori_loop(0, HALF, finish_head, 0, unroll=2)
    mine[1] = at[1 - t].astype(BF16)
    trade = remote(mine.at[1], theirs, ss.at[10], rx_sem.at[0], sib)
    trade.start()
    mine[0] = at[t].astype(BF16)
    out_w[0].wait()
    out_w[1].wait()

    @pl.when(moved)
    def _():
        swap_z.wait_recv()
        swap_dz.wait_recv()

    trade.wait_recv()
    pl.semaphore_wait(relay.at[3], 1)

    def forward(q, n):
        a, b, d = OFFSETS[n]
        to = (lax.rem(zh + a, 2), lax.rem(y + b, 4), c, lax.rem(zl + d, 2), x)
        return remote(
            tx.at[q, member(to[0], to[1], to[3])], rx.at[q, me], fs.at[16 * q + n], fr.at[16 * q + n], to
        )

    def forward_own(q):
        return pltpu.make_async_copy(tx.at[q, me], rx.at[q, me], fl.at[q])

    def give_back(q, n):
        a, b, d = OFFSETS[n]
        z2, y2, l2 = lax.rem(zh + a, 2), lax.rem(y + b, 4), lax.rem(zl + d, 2)
        return remote(
            ty.at[q, member(z2, y2, l2)], got.at[q, me], gs.at[16 * q + n], gr.at[16 * q + n], (z2, y2, l2, c, x)
        )

    def give_own(q):
        return pltpu.make_async_copy(ty.at[q, me], got.at[q, me], gl.at[q])

    others = [n for n in range(16) if n != SELF]
    gate = mod_ref[2:3, :]
    dgate = dmod_ref[2:3, :]
    lo = pl.ds(pl.multiple_of(576 * c, 16), 576)
    hi = pl.ds(pl.multiple_of(576 * (1 - c), 16), 576)

    def spatial_out(q, _):
        both = dot(mine[0, q], wos[lo, :], ((0,), (0,))) + dot(theirs[q], wos[hi, :], ((0,), (0,)))
        rows = pl.ds(pl.multiple_of(CHUNK * q, CHUNK), CHUNK)
        proj, dproj = both[0:CHUNK], both[CHUNK:]
        tx[q] = joined(
            zb[0, rows, :].astype(F32) + gate * proj,
            zb[1, rows, :].astype(F32) + gate * dproj + dgate * proj,
        )
        return 0

    def send(q):
        forward_own(q).start()
        for n in others:
            forward(q, n).start()

    spatial_out(0, 0)
    send(0)
    spatial_out(1, 0)

    ki = lax.broadcasted_iota(jnp.int32, (CHUNK, CHUNK), 0)
    qi = lax.broadcasted_iota(jnp.int32, (CHUNK, CHUNK), 1)
    place = (ki & 7) == (qi & 7)

    def temporal_chunk(q, _):
        forward_own(q).wait()
        for n in others:
            forward(q, n).wait_recv()
        pl.when(q == 0)(lambda: send(1))

        def put(at_row, rows, h, dh):
            th[pl.ds(at_row, rows), :] = h
            th[pl.ds(CHUNK + at_row, rows), :] = dh

        def half(which):
            return lambda a, n: both_halves(rx[q, pl.ds(a // 8, n // 8)].astype(F32))[which]

        normed_hidden(CHUNK, half(0), half(1), mod_ref, dmod_ref, put)
        for j in range(3):
            kt[:, 256 * j : 256 * j + 256] = dot(wtt[D * j : D * j + D, :], th[...], ((1,), (1,)))

        def one_head(h, _):
            rows = pl.ds(pl.multiple_of(h * HD, 8), HD)
            first, second = query_operands(kt[rows, 0:128], kt[rows, 128:256], gains[2])
            kd = key_operand(kt[rows, 256:384], kt[rows, 384:512], gains[3])
            ve, vg = value_operands(kt[rows, 512:640], kt[rows, 640:768])
            both = dot(kd, jnp.concatenate([first, second], 1), ((1,), (0,)))
            s = jnp.where(place, both[:, 0:128], -1e30)
            e = jnp.exp2(s - jnp.max(s, 0, keepdims=True))
            g = e * both[:, 128:256]
            of_e = dot(ve, e.astype(BF16), ((1,), (0,)))
            of_g = dot(vg, g.astype(BF16), ((1,), (0,)))
            inv = 1.0 / of_e[144:145]
            attn = of_e[0:72] * inv
            dattn = (of_e[72:144] + of_g[0:72] - of_g[73:74] * attn) * inv
            to_rows = pl.ds(pl.multiple_of(lax.rem(h, 8) * HD, 8), HD)
            at[0, h // 8, to_rows, 0:128] = attn
            at[0, h // 8, to_rows, 128:256] = dattn
            return 0

        lax.fori_loop(0, HEADS, one_head, 0, unroll=4)
        both = dot(at[0, 0].astype(BF16), wot[0:576, :], ((0,), (0,)))
        both += dot(at[0, 1].astype(BF16), wot[576:1152, :], ((0,), (0,)))
        proj, dproj = both[0:CHUNK], both[CHUNK:]
        z, dz = both_halves(rx[q].astype(F32))
        ty[q] = joined(z + gate * proj, dz + gate * dproj + dgate * proj)
        pl.when(same)(lambda: give_own(q).start())
        pl.when(moved)(lambda: give_back(q, SELF).start())
        for n in others:
            give_back(q, n).start()
        return 0

    lax.fori_loop(0, 2, temporal_chunk, 0)

    def collect(q, _):
        pl.when(same)(lambda: give_own(q).wait())
        pl.when(moved)(lambda: give_back(q, SELF).wait())
        for n in others:
            give_back(q, n).wait()
            forward(q, n).wait_send()
        rows = pl.ds(pl.multiple_of(CHUNK * q, CHUNK), CHUNK)
        z, dz = both_halves(got[q].astype(F32))
        out_ref[0, rows, :] = z.astype(BF16)
        out_ref[1, rows, :] = dz.astype(BF16)
        return 0

    lax.fori_loop(0, 2, collect, 0)

    for copy in (to_right, to_left, *to_sib, on_left, on_right, trade):
        copy.wait_send()

    @pl.when(moved)
    def _():
        for copy in (*swaps, swap_z, swap_dz):
            copy.wait_send()


def split_kernel(both_ref, out_ref, dout_ref):
    out_ref[...] = both_ref[0]
    dout_ref[...] = both_ref[1]


def body(
    latent,
    latent_tangent,
    modulation,
    modulation_tangent,
    w_qkv_s,
    w_out_s,
    q_gain_s,
    k_gain_s,
    w_qkv_t,
    w_out_t,
    q_gain_t,
    k_gain_t,
):
    shape = latent.shape
    vmem = pl.BlockSpec(memory_space=pltpu.VMEM)
    hbm = pl.BlockSpec(memory_space=pl.ANY)
    dma = pltpu.SemaphoreType.DMA
    one = jax.ShapeDtypeStruct((TOK, D), BF16)
    row = lambda gain: gain.reshape(1, HD)
    both = pl.pallas_call(
        block_kernel,
        out_shape=jax.ShapeDtypeStruct((2, TOK, D), BF16),
        in_specs=[vmem, vmem, vmem, vmem, hbm, hbm, vmem, vmem, hbm, hbm, vmem, vmem],
        out_specs=vmem,
        scratch_shapes=[
            pltpu.VMEM((9, 2, TOK, D), BF16),
            pltpu.VMEM((2, TOK, D), BF16),
            pltpu.VMEM((2, D, 640), BF16),
            pltpu.VMEM((640, D), BF16),
            pltpu.VMEM((1728, D), BF16),
            pltpu.VMEM((D, D), BF16),
            pltpu.VMEM((3 * D, D), BF16),
            pltpu.VMEM((D, D), BF16),
            pltpu.VMEM((D, 4 * TOK), F32),
            pltpu.VMEM((HALF, 144, 2 * TOK), BF16),
            pltpu.VMEM((HALF, 144, 2 * TOK), BF16),
            pltpu.VMEM((HALF, 2 * TOK, 144), BF16),
            pltpu.VMEM((HALF, 160, 2 * TOK), BF16),
            pltpu.VMEM((HALF, 80, 2 * TOK), BF16),
            pltpu.VMEM((HALF, 160, 2 * TOK), F32),
            pltpu.VMEM((HALF, 8, 2 * TOK), F32),
            pltpu.VMEM((2, 2, 576, TOK), F32),
            pltpu.VMEM((2, 2, 576, TOK), BF16),
            pltpu.VMEM((2, 576, TOK), BF16),
            pltpu.VMEM((TOK, D), BF16),
            pltpu.VMEM((2, 16, 16, D), BF16),
            pltpu.VMEM((2, 16, 16, D), BF16),
            pltpu.VMEM((2, 16, 16, D), BF16),
            pltpu.VMEM((2, 16, 16, D), BF16),
            pltpu.VMEM((4, HD, 1), F32),
            pltpu.SemaphoreType.REGULAR((4,)),
            dma((2,)), dma((2,)), dma((5,)), dma((4,)), dma((2,)), dma((1,)), dma((11,)),
            dma((4,)), dma((4,)),
            dma((32,)), dma((32,)), dma((2,)), dma((32,)), dma((32,)), dma((2,)),
        ],
        compiler_params=pltpu.CompilerParams(
            collective_id=1, has_side_effects=True, vmem_limit_bytes=63 * 2**20
        ),
        cost_estimate=pl.CostEstimate(flops=53_000_000_000, bytes_accessed=25_000_000, transcendentals=9_000_000),
        name="blocks",
    )(
        latent.reshape(TOK, D), latent_tangent.reshape(TOK, D), modulation, modulation_tangent,
        w_qkv_s, w_out_s, row(q_gain_s), row(k_gain_s), w_qkv_t, w_out_t, row(q_gain_t), row(k_gain_t),
    )
    out, dout = pl.pallas_call(
        split_kernel,
        out_shape=(one, one),
        in_specs=[vmem],
        out_specs=(vmem, vmem),
        name="results",
    )(both)
    return out.reshape(shape), dout.reshape(shape)


def solution(mesh):
    split = Mesh(mesh.devices.reshape(2, 4, 2, 2, 4), AXES)
    tokens = P(("zh", "y", "core"), ("zl", "x"), None, None)
    return jax.shard_map(
        body, mesh=split, in_specs=(tokens, tokens) + (P(),) * 10, out_specs=(tokens, tokens), check_vma=False
    )
```

```python
import functools
import math

import jax
import jax.numpy as jnp
from jax import lax
from jax.experimental import pallas as pl
from jax.experimental.pallas import tpu as pltpu
from jax.sharding import Mesh, PartitionSpec as P

D = 1152
HEADS = 16
HD = 72
EPS = 1e-06
AXES = ("zh", "y", "core", "zl", "x")
TOK = 256
HALF = 8
FACTOR = 1.0 / math.sqrt(HD)
LOG2E = 1.4426950408889634
MESH = pl.DeviceIdType.MESH
F32 = jnp.float32
BF16 = jnp.bfloat16


def coords():
    return tuple(lax.axis_index(a) for a in AXES)


def dot(a, b, dims):
    return lax.dot_general(a, b, (dims, ((), ())), preferred_element_type=F32)


def normed_hidden(count, z_of, dz_of, mod_ref, dmod_ref, put):
    rows = 32

    def step(i, _):
        at = pl.multiple_of(i * rows, rows)
        z = z_of(at, rows).astype(F32)
        dz = dz_of(at, rows).astype(F32)
        cent = z - jnp.mean(z, -1, keepdims=True)
        rstd = lax.rsqrt(jnp.mean(cent * cent, -1, keepdims=True) + EPS)
        normed = cent * rstd
        dcent = dz - jnp.mean(dz, -1, keepdims=True)
        dnormed = rstd * (dcent - normed * jnp.mean(normed * dcent, -1, keepdims=True))
        scale = 1.0 + mod_ref[1:2, :]
        hidden = normed * scale + mod_ref[0:1, :]
        dhidden = dnormed * scale + normed * dmod_ref[1:2, :] + dmod_ref[0:1, :]
        put(at, rows, hidden.astype(BF16), dhidden.astype(BF16))
        return 0

    lax.fori_loop(0, count // rows, step, 0)


def head_norm(u, du):
    r = lax.rsqrt(jnp.mean(u * u, 0, keepdims=True) + EPS)
    unit = u * r
    return unit, r * (du - unit * jnp.mean(unit * du, 0, keepdims=True))


def query_operands(q, dq, gain):
    unit, inner = head_norm(q, dq)
    qn = unit * (gain * FACTOR)
    dqn = inner * (gain * FACTOR)
    first = jnp.concatenate([qn * LOG2E, jnp.zeros_like(qn)], 0).astype(BF16)
    second = jnp.concatenate([dqn, qn], 0).astype(BF16)
    return first, second


def key_operand(k, dk, gain):
    unit, inner = head_norm(k, dk)
    both = jnp.concatenate([unit * gain, inner * gain], 0)
    return both.T.astype(BF16)


def value_operands(v, dv):
    n = v.shape[1]
    row16 = lax.broadcasted_iota(jnp.int32, (16, n), 0)
    row8 = lax.broadcasted_iota(jnp.int32, (8, n), 0)
    for_e = jnp.concatenate([v, dv, (row16 == 0).astype(F32)], 0).astype(BF16)
    for_g = jnp.concatenate([v, (row8 == 1).astype(F32)], 0).astype(BF16)
    return for_e, for_g


def normalised(acc):
    inv = 1.0 / acc[144:145]
    attn = acc[0:72] * inv
    dattn = (acc[72:144] - acc[145:146] * attn) * inv
    return attn, dattn


OFFSETS = sorted(
    ((a, b, d) for a in (0, 1) for b in (2, 0, 1, 3) for d in (1, 0)),
    key=lambda o: -((1 if o[2] else 2 * o[0]) + min(o[1], 4 - o[1])),
)
SELF = OFFSETS.index((0, 0, 0))
CHUNK = 128


def member(zh, y, zl):
    return (zh * 4 + y) * 2 + zl


def both_halves(x):
    n = x.shape[0] * 8
    return x[:, 0:8].reshape(n, D), x[:, 8:16].reshape(n, D)


def joined(z, dz):
    n = z.shape[0] // 8
    return jnp.concatenate([z.reshape(n, 8, D), dz.reshape(n, 8, D)], 1).astype(BF16)


def block_kernel(
    z_ref, dz_ref, mod_ref, dmod_ref, wqkv_s, wout_s, qg_s, kg_s, wqkv_t, wout_t, qg_t, kg_t,
    got,
    hb, zb, stage, wtmp, wt, wos, wtt, wot, kt, qs, qd, kds, ves, vgs, acc, mx, at, mine, theirs,
    th, tx, rx, ty, gains,
    relay, stage_sem, wsem, ro, rb, rz, rx_sem, ss, sw_s, sw_r, fs, fr, fl, gs, gr, gl,
):
    zh, y, c, zl, x = coords()
    right = (zh, y, c, zl, lax.rem(x + 1, 4))
    left = (zh, y, c, zl, lax.rem(x + 3, 4))
    sib = (zh, y, 1 - c, zl, x)
    partner = (zh, y, zl, c, x)
    t = lax.rem(c + zl, 2)
    me = member(zh, y, zl)
    same = t == 0
    moved = t == 1

    barrier = pltpu.get_barrier_semaphore()

    def greet(peer):
        pl.semaphore_signal(barrier, inc=1, device_id=peer, device_id_type=MESH)

    z = 2 * zh + zl

    def at_z(n):
        zz = lax.rem(z + n, 4)
        return (zz // 2, y, c, lax.rem(zz, 2), x)

    plane = [(zh, lax.rem(y + n, 4), c, zl, x) for n in (1, 3)] + [at_z(1), at_z(3)]
    for peer in (right, left, sib, *plane):
        greet(peer)
    pl.when(moved)(lambda: greet(partner))

    def tell(n):
        for peer in plane:
            pl.semaphore_signal(relay.at[n], inc=1, device_id=peer, device_id_type=MESH)

    def hear(n):
        pl.semaphore_wait(relay.at[n], 4)

    out_w = [pltpu.make_async_copy(wout_s, wos, wsem.at[0]), pltpu.make_async_copy(wout_t, wot, wsem.at[1])]

    def window(j):
        cols = pl.ds(pl.multiple_of(D * j + 512 * c, 128), 640)
        return pltpu.make_async_copy(wqkv_s.at[:, cols], stage.at[j % 2], stage_sem.at[j % 2])

    def piece(i, slot):
        cols = pl.ds(pl.multiple_of(384 * i, 128), 384)
        return pltpu.make_async_copy(wqkv_t.at[:, cols], stage.at[slot, :, pl.ds(0, 384)], stage_sem.at[slot])

    window(0).start()
    window(1).start()
    for copy in out_w:
        copy.start()

    def remote(src, dst, send, recv, to):
        return pltpu.make_async_remote_copy(
            src_ref=src, dst_ref=dst, send_sem=send, recv_sem=recv, device_id=to, device_id_type=MESH
        )

    def slot(dx):
        return hb.at[2 * dx + t]

    to_right = remote(slot(0), slot(3), ss.at[0], ro.at[3], right)
    to_left = remote(slot(0), slot(1), ss.at[1], ro.at[1], left)
    to_sib = [remote(slot(dx), slot(dx), ss.at[2 + dx], rb.at[dx], sib) for dx in range(4)]
    on_left = remote(slot(1).at[0], slot(2).at[0], ss.at[6], ro.at[2], left)
    on_right = remote(slot(3).at[1], slot(2).at[1], ss.at[7], ro.at[4], right)
    swaps = [
        remote(hb.at[8, :, pl.ds(64 * q, 64)], hb.at[1, :, pl.ds(64 * q, 64)], sw_s.at[q], sw_r.at[q], partner)
        for q in range(4)
    ]
    swap_z = remote(z_ref, zb.at[0], ss.at[8], rz.at[0], partner)
    swap_dz = remote(dz_ref, zb.at[1], ss.at[9], rz.at[1], partner)

    own = 8 * t
    for q in range(4):

        def put(at_row, rows, h, dh):
            hb[own, 0, pl.ds(64 * q + at_row, rows), :] = h
            hb[own, 1, pl.ds(64 * q + at_row, rows), :] = dh

        normed_hidden(
            64,
            lambda a, n: z_ref[pl.ds(64 * q + a, n), :],
            lambda a, n: dz_ref[pl.ds(64 * q + a, n), :],
            mod_ref, dmod_ref, put,
        )
        if q == 0:
            pl.when(same)(lambda: pl.semaphore_wait(barrier, 7))
            pl.when(moved)(lambda: pl.semaphore_wait(barrier, 8))
        pl.when(moved)(swaps[q].start)

    @pl.when(same)
    def _():
        to_sib[0].start()
        to_right.start()
        to_left.start()
        zb[0] = z_ref[...]
        zb[1] = dz_ref[...]

    tell(0)

    for j in range(3):
        window(j).wait()
        for i in range(5):
            wtmp[pl.ds(128 * i, 128), :] = stage[j % 2, :, pl.ds(128 * i, 128)].T
        if j == 0:
            window(2).start()
        else:
            piece(j - 1, j % 2).start()
        wt[pl.ds(576 * j, 576), :] = wtmp[pl.ds(pl.multiple_of(64 * c, 64), 576), :]

    hear(0)
    tell(1)

    for i, g in enumerate((qg_s, kg_s, qg_t, kg_t)):
        rows = lax.broadcasted_iota(jnp.int32, (HD, HD), 0)
        cols = lax.broadcasted_iota(jnp.int32, (HD, HD), 1)
        gains[i] = jnp.sum(jnp.where(rows == cols, g[...], 0.0), 1, keepdims=True)

    acc[...] = jnp.zeros_like(acc)
    mx[...] = jnp.full_like(mx, -1e30)

    def turn_piece(i, _):
        which = lax.rem(i + 1, 2)
        piece(i, which).wait()
        for n in range(3):
            rows = pl.ds(pl.multiple_of(384 * i + 128 * n, 128), 128)
            wtt[rows, :] = stage[which, :, pl.ds(128 * n, 128)].T

        @pl.when(i < 7)
        def _():
            piece(i + 2, which).start()

        return 0

    lax.fori_loop(0, 9, turn_piece, 0)
    hear(1)
    tell(2)

    def query_rows(part):
        kt[0:576, 0:512] = dot(wt[0:576, :], hb[part].reshape(2 * TOK, D), ((1,), (1,)))

        def make_query(h, _):
            rows = pl.ds(pl.multiple_of(h * HD, 8), HD)
            first, second = query_operands(kt[rows, 0:256], kt[rows, 256:512], gains[0])
            qs[h, :, 256 * part : 256 * part + 256] = first
            qd[h, :, 256 * part : 256 * part + 256] = second
            return 0

        lax.fori_loop(0, HALF, make_query, 0, unroll=4)

    pl.when(moved)(to_sib[0].wait_recv)
    query_rows(0)

    @pl.when(moved)
    def _():
        for copy in swaps:
            copy.wait_recv()
        to_sib[0].start()
        to_right.start()
        to_left.start()
        swap_z.start()
        swap_dz.start()

    @pl.when(same)
    def _():
        to_left.wait_recv()
        on_left.start()
        to_sib[1].start()
        to_right.wait_recv()
        on_right.start()
        to_sib[3].start()
        to_sib[0].wait_recv()

    query_rows(1)
    hear(2)
    pl.semaphore_signal(relay.at[3], inc=1, device_id=sib, device_id_type=MESH)

    def two_shards(i, _):
        @pl.when((i == 1) & moved)
        def _():
            to_sib[1].wait_recv()
            to_sib[3].wait_recv()

        @pl.when((i == 2) & moved)
        def _():
            to_left.wait_recv()
            on_left.start()
            to_sib[1].start()
            to_right.wait_recv()
            on_right.start()
            to_sib[3].start()

        @pl.when((i == 2) & same)
        def _():
            on_left.wait_recv()
            on_right.wait_recv()
            to_sib[2].start()
            to_sib[1].wait_recv()
            to_sib[3].wait_recv()

        @pl.when((i == 3) & moved)
        def _():
            on_left.wait_recv()
            on_right.wait_recv()
            to_sib[2].start()

        @pl.when(i == 3)
        def _():
            to_sib[2].wait_recv()

        first = jnp.where(i == 0, 0, i + 1)
        second = jnp.where(i == 0, 1, jnp.where(i == 3, 5, i + 5))
        for s, index in enumerate((first, second)):
            kt[:, 512 * s : 512 * s + 512] = dot(wt[576:1728, :], hb[index].reshape(2 * TOK, D), ((1,), (1,)))

        def one_head(h, _):
            krow = pl.ds(pl.multiple_of(h * HD, 8), HD)
            vrow = pl.ds(pl.multiple_of(576 + h * HD, 8), HD)
            for s in range(2):
                o = 512 * s
                keys = slice(256 * s, 256 * s + 256)
                kds[h, keys, :] = key_operand(kt[krow, o : o + 256], kt[krow, o + 256 : o + 512], gains[1])
                ve, vg = value_operands(kt[vrow, o : o + 256], kt[vrow, o + 256 : o + 512])
                ves[h, :, keys] = ve
                vgs[h, :, keys] = vg
            kd = kds[h]
            s = dot(kd, qs[h], ((1,), (0,)))
            ds = dot(kd, qd[h], ((1,), (0,)))
            old = mx[h, 0:1, :]
            new = jnp.maximum(old, jnp.max(s, 0, keepdims=True))
            mx[h, 0:1, :] = new
            e = jnp.exp2(s - new)
            g = e * ds
            keep = jnp.exp2(old - new)
            of_e = dot(ves[h], e.astype(BF16), ((1,), (0,)))
            of_g = dot(vgs[h], g.astype(BF16), ((1,), (0,)))
            acc[h, 0:72, :] = acc[h, 0:72, :] * keep + of_e[0:72]
            acc[h, 72:152, :] = acc[h, 72:152, :] * keep + of_e[72:152] + of_g
            return 0

        lax.fori_loop(0, HALF, one_head, 0, unroll=8)
        return 0

    lax.fori_loop(0, 4, two_shards, 0)

    def finish_head(h, _):
        attn, dattn = normalised(acc[h])
        rows = pl.ds(pl.multiple_of(h * HD, 8), HD)
        for part in range(2):
            for q in range(2):
                cols = slice(256 * part + 128 * q, 256 * part + 128 * q + 128)
                at[part, q, rows, 0:128] = attn[:, cols]
                at[part, q, rows, 128:256] = dattn[:, cols]
        return 0

    lax.fori_loop(0, HALF, finish_head, 0, unroll=2)
    mine[1] = at[1 - t].astype(BF16)
    trade = remote(mine.at[1], theirs, ss.at[10], rx_sem.at[0], sib)
    trade.start()
    mine[0] = at[t].astype(BF16)
    out_w[0].wait()
    out_w[1].wait()
    lo = pl.ds(pl.multiple_of(576 * c, 16), 576)
    hi = pl.ds(pl.multiple_of(576 * (1 - c), 16), 576)

    def own_heads(q):
        return dot(mine[0, q], wos[lo, :], ((0,), (0,)))

    own_part = own_heads(0)

    @pl.when(moved)
    def _():
        swap_z.wait_recv()
        swap_dz.wait_recv()

    trade.wait_recv()
    pl.semaphore_wait(relay.at[3], 1)

    def forward(q, n):
        a, b, d = OFFSETS[n]
        to = (lax.rem(zh + a, 2), lax.rem(y + b, 4), c, lax.rem(zl + d, 2), x)
        return remote(
            tx.at[q, member(to[0], to[1], to[3])], rx.at[q, me], fs.at[16 * q + n], fr.at[16 * q + n], to
        )

    def forward_own(q):
        return pltpu.make_async_copy(tx.at[q, me], rx.at[q, me], fl.at[q])

    def give_back(q, n):
        a, b, d = OFFSETS[n]
        z2, y2, l2 = lax.rem(zh + a, 2), lax.rem(y + b, 4), lax.rem(zl + d, 2)
        return remote(
            ty.at[q, member(z2, y2, l2)], got.at[q, me], gs.at[16 * q + n], gr.at[16 * q + n], (z2, y2, l2, c, x)
        )

    def give_own(q):
        return pltpu.make_async_copy(ty.at[q, me], got.at[q, me], gl.at[q])

    others = [n for n in range(16) if n != SELF]
    gate = mod_ref[2:3, :]
    dgate = dmod_ref[2:3, :]

    def spatial_out(q, part):
        both = part + dot(theirs[q], wos[hi, :], ((0,), (0,)))
        rows = pl.ds(CHUNK * q, CHUNK)
        proj, dproj = both[0:CHUNK], both[CHUNK:]
        tx[q] = joined(
            zb[0, rows, :].astype(F32) + gate * proj,
            zb[1, rows, :].astype(F32) + gate * dproj + dgate * proj,
        )

    def send(q):
        forward_own(q).start()
        for n in others:
            forward(q, n).start()

    spatial_out(0, own_part)
    send(0)
    spatial_out(1, own_heads(1))

    ki = lax.broadcasted_iota(jnp.int32, (CHUNK, CHUNK), 0)
    qi = lax.broadcasted_iota(jnp.int32, (CHUNK, CHUNK), 1)
    place = (ki & 7) == (qi & 7)

    def temporal_chunk(q, _):
        forward_own(q).wait()
        for n in others:
            forward(q, n).wait_recv()
        pl.when(q == 0)(lambda: send(1))

        def put(at_row, rows, h, dh):
            th[pl.ds(at_row, rows), :] = h
            th[pl.ds(CHUNK + at_row, rows), :] = dh

        def half(which):
            return lambda a, n: both_halves(rx[q, pl.ds(a // 8, n // 8)].astype(F32))[which]

        normed_hidden(CHUNK, half(0), half(1), mod_ref, dmod_ref, put)
        for j in range(3):
            kt[:, 256 * j : 256 * j + 256] = dot(wtt[D * j : D * j + D, :], th[...], ((1,), (1,)))

        def one_head(h, _):
            rows = pl.ds(pl.multiple_of(h * HD, 8), HD)
            first, second = query_operands(kt[rows, 0:128], kt[rows, 128:256], gains[2])
            kd = key_operand(kt[rows, 256:384], kt[rows, 384:512], gains[3])
            ve = value_operands(kt[rows, 512:640], kt[rows, 640:768])[0]
            both = dot(kd, jnp.concatenate([first, second], 1), ((1,), (0,)))
            s = jnp.where(place, both[:, 0:128], -1e30)
            e = jnp.exp2(s - jnp.max(s, 0, keepdims=True))
            g = e * both[:, 128:256]
            sums = dot(ve, jnp.concatenate([e, g], 1).astype(BF16), ((1,), (0,)))
            of_e, of_g = sums[:, 0:128], sums[:, 128:256]
            inv = 1.0 / of_e[144:145]
            attn = of_e[0:72] * inv
            dattn = (of_e[72:144] + of_g[0:72] - of_g[144:145] * attn) * inv
            to_rows = pl.ds(pl.multiple_of(lax.rem(h, 8) * HD, 8), HD)
            at[0, h // 8, to_rows, 0:128] = attn
            at[0, h // 8, to_rows, 128:256] = dattn
            return 0

        lax.fori_loop(0, HEADS, one_head, 0, unroll=4)
        both = dot(at[0, 0].astype(BF16), wot[0:576, :], ((0,), (0,)))
        both += dot(at[0, 1].astype(BF16), wot[576:1152, :], ((0,), (0,)))
        proj, dproj = both[0:CHUNK], both[CHUNK:]
        z, dz = both_halves(rx[q].astype(F32))
        ty[q] = joined(z + gate * proj, dz + gate * dproj + dgate * proj)
        pl.when(same)(lambda: give_own(q).start())
        pl.when(moved)(lambda: give_back(q, SELF).start())
        for n in others:
            give_back(q, n).start()
        return 0

    lax.fori_loop(0, 2, temporal_chunk, 0)

    def collect(q, _):
        pl.when(same)(lambda: give_own(q).wait())
        pl.when(moved)(lambda: give_back(q, SELF).wait())
        for n in others:
            give_back(q, n).wait()
            forward(q, n).wait_send()
        return 0

    lax.fori_loop(0, 2, collect, 0)

    for copy in (to_right, to_left, *to_sib, on_left, on_right, trade):
        copy.wait_send()

    @pl.when(moved)
    def _():
        for copy in (*swaps, swap_z, swap_dz):
            copy.wait_send()


def split_kernel(both_ref, out_ref, dout_ref):
    for q in range(2):
        z, dz = both_halves(both_ref[q].astype(F32))
        out_ref[CHUNK * q : CHUNK * (q + 1), :] = z.astype(BF16)
        dout_ref[CHUNK * q : CHUNK * (q + 1), :] = dz.astype(BF16)


def body(
    latent,
    latent_tangent,
    modulation,
    modulation_tangent,
    w_qkv_s,
    w_out_s,
    q_gain_s,
    k_gain_s,
    w_qkv_t,
    w_out_t,
    q_gain_t,
    k_gain_t,
):
    shape = latent.shape
    vmem = pl.BlockSpec(memory_space=pltpu.VMEM)
    hbm = pl.BlockSpec(memory_space=pl.ANY)
    dma = pltpu.SemaphoreType.DMA
    one = jax.ShapeDtypeStruct((TOK, D), BF16)
    row = lambda gain: gain.reshape(1, HD)
    both = pl.pallas_call(
        block_kernel,
        out_shape=jax.ShapeDtypeStruct((2, 16, 16, D), BF16),
        in_specs=[vmem, vmem, vmem, vmem, hbm, hbm, vmem, vmem, hbm, hbm, vmem, vmem],
        out_specs=vmem,
        scratch_shapes=[
            pltpu.VMEM((9, 2, TOK, D), BF16),
            pltpu.VMEM((2, TOK, D), BF16),
            pltpu.VMEM((2, D, 640), BF16),
            pltpu.VMEM((640, D), BF16),
            pltpu.VMEM((1728, D), BF16),
            pltpu.VMEM((D, D), BF16),
            pltpu.VMEM((3 * D, D), BF16),
            pltpu.VMEM((D, D), BF16),
            pltpu.VMEM((D, 4 * TOK), F32),
            pltpu.VMEM((HALF, 144, 2 * TOK), BF16),
            pltpu.VMEM((HALF, 144, 2 * TOK), BF16),
            pltpu.VMEM((HALF, 2 * TOK, 144), BF16),
            pltpu.VMEM((HALF, 160, 2 * TOK), BF16),
            pltpu.VMEM((HALF, 80, 2 * TOK), BF16),
            pltpu.VMEM((HALF, 160, 2 * TOK), F32),
            pltpu.VMEM((HALF, 8, 2 * TOK), F32),
            pltpu.VMEM((2, 2, 576, TOK), F32),
            pltpu.VMEM((2, 2, 576, TOK), BF16),
            pltpu.VMEM((2, 576, TOK), BF16),
            pltpu.VMEM((TOK, D), BF16),
            pltpu.VMEM((2, 16, 16, D), BF16),
            pltpu.VMEM((2, 16, 16, D), BF16),
            pltpu.VMEM((2, 16, 16, D), BF16),
            pltpu.VMEM((4, HD, 1), F32),
            pltpu.SemaphoreType.REGULAR((4,)),
            dma((2,)), dma((2,)), dma((5,)), dma((4,)), dma((2,)), dma((1,)), dma((11,)),
            dma((4,)), dma((4,)),
            dma((32,)), dma((32,)), dma((2,)), dma((32,)), dma((32,)), dma((2,)),
        ],
        compiler_params=pltpu.CompilerParams(
            collective_id=1, has_side_effects=True, vmem_limit_bytes=63 * 2**20
        ),
        cost_estimate=pl.CostEstimate(flops=53_000_000_000, bytes_accessed=25_000_000, transcendentals=9_000_000),
        name="blocks",
    )(
        latent.reshape(TOK, D), latent_tangent.reshape(TOK, D), modulation, modulation_tangent,
        w_qkv_s, w_out_s, row(q_gain_s), row(k_gain_s), w_qkv_t, w_out_t, row(q_gain_t), row(k_gain_t),
    )
    out, dout = pl.pallas_call(
        split_kernel,
        out_shape=(one, one),
        in_specs=[vmem],
        out_specs=(vmem, vmem),
        name="results",
    )(both)
    return out.reshape(shape), dout.reshape(shape)


def solution(mesh):
    split = Mesh(mesh.devices.reshape(2, 4, 2, 2, 4), AXES)
    tokens = P(("zh", "y", "core"), ("zl", "x"), None, None)
    return jax.shard_map(
        body, mesh=split, in_specs=(tokens, tokens) + (P(),) * 10, out_specs=(tokens, tokens), check_vma=False
    )
```

```python
import functools
import math

import jax
import jax.numpy as jnp
from jax import lax
from jax.experimental import pallas as pl
from jax.experimental.pallas import tpu as pltpu
from jax.sharding import Mesh, PartitionSpec as P

D = 1152
HEADS = 16
HD = 72
EPS = 1e-06
AXES = ("zh", "y", "core", "zl", "x")
TOK = 256
HALF = 8
FACTOR = 1.0 / math.sqrt(HD)
LOG2E = 1.4426950408889634
MESH = pl.DeviceIdType.MESH
F32 = jnp.float32
BF16 = jnp.bfloat16


def coords():
    return tuple(lax.axis_index(a) for a in AXES)


def dot(a, b, dims):
    return lax.dot_general(a, b, (dims, ((), ())), preferred_element_type=F32)


def normed_hidden(count, z_of, dz_of, mod_ref, dmod_ref, put):
    rows = 32

    def step(i, _):
        at = pl.multiple_of(i * rows, rows)
        z = z_of(at, rows).astype(F32)
        dz = dz_of(at, rows).astype(F32)
        cent = z - jnp.mean(z, -1, keepdims=True)
        rstd = lax.rsqrt(jnp.mean(cent * cent, -1, keepdims=True) + EPS)
        normed = cent * rstd
        dcent = dz - jnp.mean(dz, -1, keepdims=True)
        dnormed = rstd * (dcent - normed * jnp.mean(normed * dcent, -1, keepdims=True))
        scale = 1.0 + mod_ref[1:2, :]
        hidden = normed * scale + mod_ref[0:1, :]
        dhidden = dnormed * scale + normed * dmod_ref[1:2, :] + dmod_ref[0:1, :]
        put(at, rows, hidden.astype(BF16), dhidden.astype(BF16))
        return 0

    lax.fori_loop(0, count // rows, step, 0, unroll=2)


def head_norm(u, du):
    r = lax.rsqrt(jnp.mean(u * u, 0, keepdims=True) + EPS)
    unit = u * r
    return unit, r * (du - unit * jnp.mean(unit * du, 0, keepdims=True))


def query_operands(q, dq, gain):
    unit, inner = head_norm(q, dq)
    qn = unit * (gain * FACTOR)
    dqn = inner * (gain * FACTOR)
    first = jnp.concatenate([qn * LOG2E, jnp.zeros_like(qn)], 0).astype(BF16)
    second = jnp.concatenate([dqn, qn], 0).astype(BF16)
    return first, second


def key_operand(k, dk, gain):
    unit, inner = head_norm(k, dk)
    both = jnp.concatenate([unit * gain, inner * gain], 0)
    return both.T.astype(BF16)


def value_operands(v, dv):
    n = v.shape[1]
    row16 = lax.broadcasted_iota(jnp.int32, (16, n), 0)
    row8 = lax.broadcasted_iota(jnp.int32, (8, n), 0)
    for_e = jnp.concatenate([v, dv, (row16 == 0).astype(F32)], 0).astype(BF16)
    for_g = jnp.concatenate([v, (row8 == 1).astype(F32)], 0).astype(BF16)
    return for_e, for_g


def normalised(acc):
    inv = 1.0 / acc[144:145]
    attn = acc[0:72] * inv
    dattn = (acc[72:144] - acc[145:146] * attn) * inv
    return attn, dattn


OFFSETS = sorted(
    ((a, b, d) for a in (0, 1) for b in (2, 0, 1, 3) for d in (1, 0)),
    key=lambda o: -((1 if o[2] else 2 * o[0]) + min(o[1], 4 - o[1])),
)
SELF = OFFSETS.index((0, 0, 0))
CHUNK = 128


def member(zh, y, zl):
    return (zh * 4 + y) * 2 + zl


def both_halves(x):
    n = x.shape[0] * 8
    return x[:, 0:8].reshape(n, D), x[:, 8:16].reshape(n, D)


def joined(z, dz):
    n = z.shape[0] // 8
    return jnp.concatenate([z.reshape(n, 8, D), dz.reshape(n, 8, D)], 1).astype(BF16)


def block_kernel(
    z_hbm, dz_hbm, mod_ref, dmod_ref, wqkv_s, wout_s, qg_s, kg_s, wqkv_t, wout_t, qg_t, kg_t,
    got,
    zin, hb, zb, stage, wtmp, wt, wos, wtt, wot, kt, qs, qd, kds, ves, vgs, acc, mx, at, mine, theirs,
    th, tx, rx, ty, gains,
    relay, zin_sem, stage_sem, wsem, ro, rb, rz, tr_s, tr_r, ss, sw_s, sw_r, fs, fr, fl, gs, gr, gl,
):
    zh, y, c, zl, x = coords()
    right = (zh, y, c, zl, lax.rem(x + 1, 4))
    left = (zh, y, c, zl, lax.rem(x + 3, 4))
    sib = (zh, y, 1 - c, zl, x)
    partner = (zh, y, zl, c, x)
    t = lax.rem(c + zl, 2)
    me = member(zh, y, zl)
    same = t == 0
    moved = t == 1

    z_ref, dz_ref = zin.at[0], zin.at[1]
    zin_copies = [
        pltpu.make_async_copy(ref, zin.at[n], zin_sem.at[n]) for n, ref in enumerate((z_hbm, dz_hbm))
    ]
    for copy in zin_copies:
        copy.start()

    barrier = pltpu.get_barrier_semaphore()

    def greet(peer):
        pl.semaphore_signal(barrier, inc=1, device_id=peer, device_id_type=MESH)

    z = 2 * zh + zl

    def at_z(n):
        zz = lax.rem(z + n, 4)
        return (zz // 2, y, c, lax.rem(zz, 2), x)

    plane = [(zh, lax.rem(y + n, 4), c, zl, x) for n in (1, 3)] + [at_z(1), at_z(3)]
    for peer in (right, left, sib, *plane):
        greet(peer)
    pl.when(moved)(lambda: greet(partner))

    def tell(n):
        for peer in plane:
            pl.semaphore_signal(relay.at[n], inc=1, device_id=peer, device_id_type=MESH)

    def hear(n):
        pl.semaphore_wait(relay.at[n], 4)

    out_w = [pltpu.make_async_copy(wout_s, wos, wsem.at[0]), pltpu.make_async_copy(wout_t, wot, wsem.at[1])]

    def window(j):
        cols = pl.ds(pl.multiple_of(D * j + 512 * c, 128), 640)
        return pltpu.make_async_copy(wqkv_s.at[:, cols], stage.at[j % 2], stage_sem.at[j % 2])

    def piece(i, slot):
        cols = pl.ds(pl.multiple_of(384 * i, 128), 384)
        return pltpu.make_async_copy(wqkv_t.at[:, cols], stage.at[slot, :, pl.ds(0, 384)], stage_sem.at[slot])

    window(0).start()
    window(1).start()
    for copy in out_w:
        copy.start()

    def remote(src, dst, send, recv, to):
        return pltpu.make_async_remote_copy(
            src_ref=src, dst_ref=dst, send_sem=send, recv_sem=recv, device_id=to, device_id_type=MESH
        )

    def slot(dx):
        return hb.at[2 * dx + t]

    to_right = remote(slot(0), slot(3), ss.at[0], ro.at[3], right)
    to_left = remote(slot(0), slot(1), ss.at[1], ro.at[1], left)
    to_sib = [remote(slot(dx), slot(dx), ss.at[2 + dx], rb.at[dx], sib) for dx in range(4)]
    on_left = remote(slot(1).at[0], slot(2).at[0], ss.at[6], ro.at[2], left)
    on_right = remote(slot(3).at[1], slot(2).at[1], ss.at[7], ro.at[4], right)
    swaps = [
        remote(hb.at[8, :, pl.ds(64 * q, 64)], hb.at[1, :, pl.ds(64 * q, 64)], sw_s.at[q], sw_r.at[q], partner)
        for q in range(4)
    ]
    swap_z = remote(z_ref, zb.at[0], ss.at[8], rz.at[0], partner)
    swap_dz = remote(dz_ref, zb.at[1], ss.at[9], rz.at[1], partner)

    own = 8 * t
    for copy in zin_copies:
        copy.wait()
    for q in range(4):

        def put(at_row, rows, h, dh):
            hb[own, 0, pl.ds(64 * q + at_row, rows), :] = h
            hb[own, 1, pl.ds(64 * q + at_row, rows), :] = dh

        normed_hidden(
            64,
            lambda a, n: z_ref[pl.ds(64 * q + a, n), :],
            lambda a, n: dz_ref[pl.ds(64 * q + a, n), :],
            mod_ref, dmod_ref, put,
        )
        if q == 0:
            pl.when(same)(lambda: pl.semaphore_wait(barrier, 7))
            pl.when(moved)(lambda: pl.semaphore_wait(barrier, 8))
        pl.when(moved)(swaps[q].start)

    @pl.when(same)
    def _():
        to_sib[0].start()
        to_right.start()
        to_left.start()
        zb[0] = z_ref[...]
        zb[1] = dz_ref[...]

    tell(0)

    for j in range(3):
        window(j).wait()
        for i in range(5):
            wtmp[pl.ds(128 * i, 128), :] = stage[j % 2, :, pl.ds(128 * i, 128)].T
        if j == 0:
            window(2).start()
        else:
            piece(j - 1, j % 2).start()
        wt[pl.ds(576 * j, 576), :] = wtmp[pl.ds(pl.multiple_of(64 * c, 64), 576), :]

    hear(0)
    tell(1)

    for i, g in enumerate((qg_s, kg_s, qg_t, kg_t)):
        rows = lax.broadcasted_iota(jnp.int32, (HD, HD), 0)
        cols = lax.broadcasted_iota(jnp.int32, (HD, HD), 1)
        gains[i] = jnp.sum(jnp.where(rows == cols, g[...], 0.0), 1, keepdims=True)

    acc[...] = jnp.zeros_like(acc)
    mx[...] = jnp.full_like(mx, -1e30)

    def turn_piece(i, _):
        which = lax.rem(i + 1, 2)
        piece(i, which).wait()
        for n in range(3):
            rows = pl.ds(pl.multiple_of(384 * i + 128 * n, 128), 128)
            wtt[rows, :] = stage[which, :, pl.ds(128 * n, 128)].T

        @pl.when(i < 7)
        def _():
            piece(i + 2, which).start()

        return 0

    lax.fori_loop(0, 9, turn_piece, 0)
    hear(1)
    tell(2)

    def query_rows(part):
        kt[0:576, 0:512] = dot(wt[0:576, :], hb[part].reshape(2 * TOK, D), ((1,), (1,)))

        def make_query(h, _):
            rows = pl.ds(pl.multiple_of(h * HD, 8), HD)
            first, second = query_operands(kt[rows, 0:256], kt[rows, 256:512], gains[0])
            for q in range(2):
                to = slice(256 * q + 128 * part, 256 * q + 128 * part + 128)
                qs[h, :, to] = first[:, 128 * q : 128 * q + 128]
                qd[h, :, to] = second[:, 128 * q : 128 * q + 128]
            return 0

        lax.fori_loop(0, HALF, make_query, 0, unroll=4)

    pl.when(moved)(to_sib[0].wait_recv)
    query_rows(0)

    @pl.when(moved)
    def _():
        for copy in swaps:
            copy.wait_recv()
        to_sib[0].start()
        to_right.start()
        to_left.start()
        swap_z.start()
        swap_dz.start()

    @pl.when(same)
    def _():
        to_left.wait_recv()
        on_left.start()
        to_sib[1].start()
        to_right.wait_recv()
        on_right.start()
        to_sib[3].start()
        to_sib[0].wait_recv()

    query_rows(1)
    hear(2)
    pl.semaphore_signal(relay.at[3], inc=1, device_id=sib, device_id_type=MESH)

    def keys_of(index, s):
        kt[:, 512 * s : 512 * s + 512] = dot(wt[576:1728, :], hb[index].reshape(2 * TOK, D), ((1,), (1,)))

    def prepare(h):
        krow = pl.ds(pl.multiple_of(h * HD, 8), HD)
        vrow = pl.ds(pl.multiple_of(576 + h * HD, 8), HD)
        for s in range(2):
            o = 512 * s
            keys = slice(256 * s, 256 * s + 256)
            kds[h, keys, :] = key_operand(kt[krow, o : o + 256], kt[krow, o + 256 : o + 512], gains[1])
            ve, vg = value_operands(kt[vrow, o : o + 256], kt[vrow, o + 256 : o + 512])
            ves[h, :, keys] = ve
            vgs[h, :, keys] = vg

    def attend(h, cols):
        kd = kds[h]
        s = dot(kd, qs[h, :, cols], ((1,), (0,)))
        ds = dot(kd, qd[h, :, cols], ((1,), (0,)))
        old = mx[h, 0:1, cols]
        new = jnp.maximum(old, jnp.max(s, 0, keepdims=True))
        mx[h, 0:1, cols] = new
        e = jnp.exp2(s - new)
        g = e * ds
        keep = jnp.exp2(old - new)
        of_e = dot(ves[h], e.astype(BF16), ((1,), (0,)))
        of_g = dot(vgs[h], g.astype(BF16), ((1,), (0,)))
        acc[h, 0:72, cols] = acc[h, 0:72, cols] * keep + of_e[0:72]
        acc[h, 72:152, cols] = acc[h, 72:152, cols] * keep + of_e[72:152] + of_g

    def heads(start, stop, cols, with_keys):
        def one_head(h, _):
            if with_keys:
                prepare(h)
            attend(h, cols)
            return 0

        lax.fori_loop(start, stop, one_head, 0, unroll=stop - start)

    def two_shards(i, _):
        @pl.when((i == 1) & moved)
        def _():
            to_sib[1].wait_recv()
            to_sib[3].wait_recv()

        @pl.when((i == 2) & moved)
        def _():
            to_left.wait_recv()
            on_left.start()
            to_sib[1].start()
            to_right.wait_recv()
            on_right.start()
            to_sib[3].start()

        @pl.when((i == 2) & same)
        def _():
            on_left.wait_recv()
            on_right.wait_recv()
            to_sib[2].start()
            to_sib[1].wait_recv()
            to_sib[3].wait_recv()

        keys_of(jnp.where(i == 0, 0, i + 1), 0)
        keys_of(jnp.where(i == 0, 1, i + 5), 1)
        heads(0, HALF, slice(0, 512), True)
        return 0

    lax.fori_loop(0, 3, two_shards, 0)

    @pl.when(moved)
    def _():
        on_left.wait_recv()
        on_right.wait_recv()
        to_sib[2].start()

    to_sib[2].wait_recv()
    keys_of(4, 0)
    keys_of(5, 1)
    heads(0, HALF, slice(0, 256), True)

    trades = [remote(mine.at[1, q], theirs.at[q], tr_s.at[q], tr_r.at[q], sib) for q in range(2)]

    def finish(q):
        def finish_head(h, _):
            attn, dattn = normalised(acc[h, :, 256 * q : 256 * q + 256])
            rows = pl.ds(pl.multiple_of(h * HD, 8), HD)
            for part in range(2):
                at[part, q, rows, 0:128] = attn[:, 128 * part : 128 * part + 128]
                at[part, q, rows, 128:256] = dattn[:, 128 * part : 128 * part + 128]
            return 0

        lax.fori_loop(0, HALF, finish_head, 0, unroll=4)
        mine[1, q] = at[1 - t, q].astype(BF16)
        trades[q].start()
        mine[0, q] = at[t, q].astype(BF16)

    lo = pl.ds(pl.multiple_of(576 * c, 16), 576)
    hi = pl.ds(pl.multiple_of(576 * (1 - c), 16), 576)

    def forward(q, n):
        a, b, d = OFFSETS[n]
        to = (lax.rem(zh + a, 2), lax.rem(y + b, 4), c, lax.rem(zl + d, 2), x)
        return remote(
            tx.at[q, member(to[0], to[1], to[3])], rx.at[q, me], fs.at[16 * q + n], fr.at[16 * q + n], to
        )

    def forward_own(q):
        return pltpu.make_async_copy(tx.at[q, me], rx.at[q, me], fl.at[q])

    def give_back(q, n):
        a, b, d = OFFSETS[n]
        z2, y2, l2 = lax.rem(zh + a, 2), lax.rem(y + b, 4), lax.rem(zl + d, 2)
        return remote(
            ty.at[q, member(z2, y2, l2)], got.at[q, me], gs.at[16 * q + n], gr.at[16 * q + n], (z2, y2, l2, c, x)
        )

    def give_own(q):
        return pltpu.make_async_copy(ty.at[q, me], got.at[q, me], gl.at[q])

    others = [n for n in range(16) if n != SELF]
    gate = mod_ref[2:3, :]
    dgate = dmod_ref[2:3, :]

    def spatial_out(q):
        both = dot(mine[0, q], wos[lo, :], ((0,), (0,)))
        trades[q].wait_recv()
        both += dot(theirs[q], wos[hi, :], ((0,), (0,)))
        rows = pl.ds(CHUNK * q, CHUNK)
        proj, dproj = both[0:CHUNK], both[CHUNK:]
        tx[q] = joined(
            zb[0, rows, :].astype(F32) + gate * proj,
            zb[1, rows, :].astype(F32) + gate * dproj + dgate * proj,
        )

    def send(q):
        forward_own(q).start()
        for n in others:
            forward(q, n).start()

    finish(0)
    heads(0, 4, slice(256, 512), False)
    out_w[0].wait()
    out_w[1].wait()

    @pl.when(moved)
    def _():
        swap_z.wait_recv()
        swap_dz.wait_recv()

    pl.semaphore_wait(relay.at[3], 1)
    spatial_out(0)
    send(0)
    heads(4, HALF, slice(256, 512), False)
    finish(1)
    spatial_out(1)
    for n in others:
        forward(0, n).wait_send()
    send(1)

    ki = lax.broadcasted_iota(jnp.int32, (CHUNK, CHUNK), 0)
    qi = lax.broadcasted_iota(jnp.int32, (CHUNK, CHUNK), 1)
    place = (ki & 7) == (qi & 7)

    def temporal_chunk(q, _):
        forward_own(q).wait()
        for n in others:
            forward(q, n).wait_recv()

        def put(at_row, rows, h, dh):
            th[pl.ds(at_row, rows), :] = h
            th[pl.ds(CHUNK + at_row, rows), :] = dh

        def half(which):
            return lambda a, n: both_halves(rx[q, pl.ds(a // 8, n // 8)].astype(F32))[which]

        normed_hidden(CHUNK, half(0), half(1), mod_ref, dmod_ref, put)
        for j in range(3):
            kt[:, 256 * j : 256 * j + 256] = dot(wtt[D * j : D * j + D, :], th[...], ((1,), (1,)))

        def one_head(h, _):
            rows = pl.ds(pl.multiple_of(h * HD, 8), HD)
            first, second = query_operands(kt[rows, 0:128], kt[rows, 128:256], gains[2])
            kd = key_operand(kt[rows, 256:384], kt[rows, 384:512], gains[3])
            ve = value_operands(kt[rows, 512:640], kt[rows, 640:768])[0]
            both = dot(kd, jnp.concatenate([first, second], 1), ((1,), (0,)))
            s = jnp.where(place, both[:, 0:128], -1e30)
            e = jnp.exp2(s - jnp.max(s, 0, keepdims=True))
            g = e * both[:, 128:256]
            sums = dot(ve, jnp.concatenate([e, g], 1).astype(BF16), ((1,), (0,)))
            of_e, of_g = sums[:, 0:128], sums[:, 128:256]
            inv = 1.0 / of_e[144:145]
            attn = of_e[0:72] * inv
            dattn = (of_e[72:144] + of_g[0:72] - of_g[144:145] * attn) * inv
            to_rows = pl.ds(pl.multiple_of(lax.rem(h, 8) * HD, 8), HD)
            at[0, h // 8, to_rows, 0:128] = attn
            at[0, h // 8, to_rows, 128:256] = dattn
            return 0

        lax.fori_loop(0, HEADS, one_head, 0, unroll=4)
        both = dot(at[0, 0].astype(BF16), wot[0:576, :], ((0,), (0,)))
        both += dot(at[0, 1].astype(BF16), wot[576:1152, :], ((0,), (0,)))
        proj, dproj = both[0:CHUNK], both[CHUNK:]
        z, dz = both_halves(rx[q].astype(F32))
        ty[q] = joined(z + gate * proj, dz + gate * dproj + dgate * proj)
        pl.when(same)(lambda: give_own(q).start())
        pl.when(moved)(lambda: give_back(q, SELF).start())
        for n in others:
            give_back(q, n).start()
        return 0

    lax.fori_loop(0, 2, temporal_chunk, 0)

    def collect(q, _):
        pl.when(same)(lambda: give_own(q).wait())
        pl.when(moved)(lambda: give_back(q, SELF).wait())
        for n in others:
            give_back(q, n).wait()
        return 0

    lax.fori_loop(0, 2, collect, 0)

    for n in others:
        forward(1, n).wait_send()
    for copy in (to_right, to_left, *to_sib, on_left, on_right, *trades):
        copy.wait_send()

    @pl.when(moved)
    def _():
        for copy in (*swaps, swap_z, swap_dz):
            copy.wait_send()


def split_kernel(both_ref, out_ref, dout_ref):
    for q in range(2):
        z, dz = both_halves(both_ref[q].astype(F32))
        out_ref[CHUNK * q : CHUNK * (q + 1), :] = z.astype(BF16)
        dout_ref[CHUNK * q : CHUNK * (q + 1), :] = dz.astype(BF16)


def body(
    latent,
    latent_tangent,
    modulation,
    modulation_tangent,
    w_qkv_s,
    w_out_s,
    q_gain_s,
    k_gain_s,
    w_qkv_t,
    w_out_t,
    q_gain_t,
    k_gain_t,
):
    shape = latent.shape
    vmem = pl.BlockSpec(memory_space=pltpu.VMEM)
    hbm = pl.BlockSpec(memory_space=pl.ANY)
    dma = pltpu.SemaphoreType.DMA
    one = jax.ShapeDtypeStruct((TOK, D), BF16)
    row = lambda gain: gain.reshape(1, HD)
    both = pl.pallas_call(
        block_kernel,
        out_shape=jax.ShapeDtypeStruct((2, 16, 16, D), BF16),
        in_specs=[hbm, hbm, vmem, vmem, hbm, hbm, vmem, vmem, hbm, hbm, vmem, vmem],
        out_specs=vmem,
        scratch_shapes=[
            pltpu.VMEM((2, TOK, D), BF16),
            pltpu.VMEM((9, 2, TOK, D), BF16),
            pltpu.VMEM((2, TOK, D), BF16),
            pltpu.VMEM((2, D, 640), BF16),
            pltpu.VMEM((640, D), BF16),
            pltpu.VMEM((1728, D), BF16),
            pltpu.VMEM((D, D), BF16),
            pltpu.VMEM((3 * D, D), BF16),
            pltpu.VMEM((D, D), BF16),
            pltpu.VMEM((D, 4 * TOK), F32),
            pltpu.VMEM((HALF, 144, 2 * TOK), BF16),
            pltpu.VMEM((HALF, 144, 2 * TOK), BF16),
            pltpu.VMEM((HALF, 2 * TOK, 144), BF16),
            pltpu.VMEM((HALF, 160, 2 * TOK), BF16),
            pltpu.VMEM((HALF, 80, 2 * TOK), BF16),
            pltpu.VMEM((HALF, 160, 2 * TOK), F32),
            pltpu.VMEM((HALF, 8, 2 * TOK), F32),
            pltpu.VMEM((2, 2, 576, TOK), F32),
            pltpu.VMEM((2, 2, 576, TOK), BF16),
            pltpu.VMEM((2, 576, TOK), BF16),
            pltpu.VMEM((TOK, D), BF16),
            pltpu.VMEM((2, 16, 16, D), BF16),
            pltpu.VMEM((2, 16, 16, D), BF16),
            pltpu.VMEM((2, 16, 16, D), BF16),
            pltpu.VMEM((4, HD, 1), F32),
            pltpu.SemaphoreType.REGULAR((4,)),
            dma((2,)), dma((2,)), dma((2,)), dma((5,)), dma((4,)), dma((2,)), dma((2,)), dma((2,)), dma((10,)),
            dma((4,)), dma((4,)),
            dma((32,)), dma((32,)), dma((2,)), dma((32,)), dma((32,)), dma((2,)),
        ],
        compiler_params=pltpu.CompilerParams(
            collective_id=1, has_side_effects=True, vmem_limit_bytes=63 * 2**20
        ),
        cost_estimate=pl.CostEstimate(flops=53_000_000_000, bytes_accessed=25_000_000, transcendentals=9_000_000),
        name="blocks",
    )(
        latent.reshape(TOK, D), latent_tangent.reshape(TOK, D), modulation, modulation_tangent,
        w_qkv_s, w_out_s, row(q_gain_s), row(k_gain_s), w_qkv_t, w_out_t, row(q_gain_t), row(k_gain_t),
    )
    out, dout = pl.pallas_call(
        split_kernel,
        out_shape=(one, one),
        in_specs=[vmem],
        out_specs=(vmem, vmem),
        name="results",
    )(both)
    return out.reshape(shape), dout.reshape(shape)


def solution(mesh):
    split = Mesh(mesh.devices.reshape(2, 4, 2, 2, 4), AXES)
    tokens = P(("zh", "y", "core"), ("zl", "x"), None, None)
    return jax.shard_map(
        body, mesh=split, in_specs=(tokens, tokens) + (P(),) * 10, out_specs=(tokens, tokens), check_vma=False
    )
```

```python
import functools
import math

import jax
import jax.numpy as jnp
from jax import lax
from jax.experimental import pallas as pl
from jax.experimental.pallas import tpu as pltpu
from jax.sharding import Mesh, PartitionSpec as P

D = 1152
HEADS = 16
HD = 72
EPS = 1e-06
AXES = ("zh", "y", "core", "zl", "x")
TOK = 256
HALF = 8
FACTOR = 1.0 / math.sqrt(HD)
LOG2E = 1.4426950408889634
MESH = pl.DeviceIdType.MESH
F32 = jnp.float32
BF16 = jnp.bfloat16


def coords():
    return tuple(lax.axis_index(a) for a in AXES)


def dot(a, b, dims):
    return lax.dot_general(a, b, (dims, ((), ())), preferred_element_type=F32)


def normed_hidden(count, z_of, dz_of, mod_ref, dmod_ref, put):
    rows = 32

    def step(i, _):
        at = pl.multiple_of(i * rows, rows)
        z = z_of(at, rows).astype(F32)
        dz = dz_of(at, rows).astype(F32)
        cent = z - jnp.mean(z, -1, keepdims=True)
        rstd = lax.rsqrt(jnp.mean(cent * cent, -1, keepdims=True) + EPS)
        normed = cent * rstd
        dcent = dz - jnp.mean(dz, -1, keepdims=True)
        dnormed = rstd * (dcent - normed * jnp.mean(normed * dcent, -1, keepdims=True))
        scale = 1.0 + mod_ref[1:2, :]
        hidden = normed * scale + mod_ref[0:1, :]
        dhidden = dnormed * scale + normed * dmod_ref[1:2, :] + dmod_ref[0:1, :]
        put(at, rows, hidden.astype(BF16), dhidden.astype(BF16))
        return 0

    lax.fori_loop(0, count // rows, step, 0, unroll=2)


def head_norm(u, du):
    r = lax.rsqrt(jnp.mean(u * u, 0, keepdims=True) + EPS)
    unit = u * r
    return unit, r * (du - unit * jnp.mean(unit * du, 0, keepdims=True))


def query_operands(q, dq, gain):
    unit, inner = head_norm(q, dq)
    qn = unit * (gain * FACTOR)
    dqn = inner * (gain * FACTOR)
    first = jnp.concatenate([qn * LOG2E, jnp.zeros_like(qn)], 0).astype(BF16)
    second = jnp.concatenate([dqn, qn], 0).astype(BF16)
    return first, second


def key_operand(k, dk, gain):
    unit, inner = head_norm(k, dk)
    both = jnp.concatenate([unit * gain, inner * gain], 0)
    return both.T.astype(BF16)


def value_operands(v, dv):
    n = v.shape[1]
    row16 = lax.broadcasted_iota(jnp.int32, (16, n), 0)
    row8 = lax.broadcasted_iota(jnp.int32, (8, n), 0)
    for_e = jnp.concatenate([v, dv, (row16 == 0).astype(F32)], 0).astype(BF16)
    for_g = jnp.concatenate([v, (row8 == 1).astype(F32)], 0).astype(BF16)
    return for_e, for_g


def normalised(acc):
    inv = 1.0 / acc[144:145]
    attn = acc[0:72] * inv
    dattn = (acc[72:144] - acc[145:146] * attn) * inv
    return attn, dattn


OFFSETS = sorted(
    ((a, b, d) for a in (0, 1) for b in (2, 0, 1, 3) for d in (1, 0)),
    key=lambda o: -((1 if o[2] else 2 * o[0]) + min(o[1], 4 - o[1])),
)
SELF = OFFSETS.index((0, 0, 0))
CHUNK = 128


def member(zh, y, zl):
    return (zh * 4 + y) * 2 + zl


def both_halves(x):
    n = x.shape[0] * 8
    return x[:, 0:8].reshape(n, D), x[:, 8:16].reshape(n, D)


def joined(z, dz):
    n = z.shape[0] // 8
    return jnp.concatenate([z.reshape(n, 8, D), dz.reshape(n, 8, D)], 1).astype(BF16)


def block_kernel(
    z_hbm, dz_hbm, mod_ref, dmod_ref, wqkv_s, wout_s, qg_s, kg_s, wqkv_t, wout_t, qg_t, kg_t,
    got,
    zin, hb, zb, stage, wtmp, wt, wos, wtt, wot, kt, qs, qd, kds, ves, vgs, acc, mx, at, mine, theirs,
    th, tx, rx, ty, gains,
    relay, zin_sem, stage_sem, wsem, ro, rb, rz, tr_s, tr_r, ss, sw_s, sw_r, fs, fr, fl, gs, gr, gl,
):
    zh, y, c, zl, x = coords()
    right = (zh, y, c, zl, lax.rem(x + 1, 4))
    left = (zh, y, c, zl, lax.rem(x + 3, 4))
    sib = (zh, y, 1 - c, zl, x)
    partner = (zh, y, zl, c, x)
    t = lax.rem(c + zl, 2)
    me = member(zh, y, zl)
    same = t == 0
    moved = t == 1

    z_ref, dz_ref = zin.at[0], zin.at[1]
    zin_copies = [
        pltpu.make_async_copy(ref, zin.at[n], zin_sem.at[n]) for n, ref in enumerate((z_hbm, dz_hbm))
    ]
    for copy in zin_copies:
        copy.start()

    barrier = pltpu.get_barrier_semaphore()

    def greet(peer):
        pl.semaphore_signal(barrier, inc=1, device_id=peer, device_id_type=MESH)

    z = 2 * zh + zl

    def at_z(n):
        zz = lax.rem(z + n, 4)
        return (zz // 2, y, c, lax.rem(zz, 2), x)

    plane = [(zh, lax.rem(y + n, 4), c, zl, x) for n in (1, 3)] + [at_z(1), at_z(3)]
    for peer in (right, left, sib, *plane):
        greet(peer)
    pl.when(moved)(lambda: greet(partner))

    def tell(n):
        for peer in plane:
            pl.semaphore_signal(relay.at[n], inc=1, device_id=peer, device_id_type=MESH)

    def hear(n):
        pl.semaphore_wait(relay.at[n], 4)

    out_w = [pltpu.make_async_copy(wout_s, wos, wsem.at[0]), pltpu.make_async_copy(wout_t, wot, wsem.at[1])]

    def window(j):
        cols = pl.ds(pl.multiple_of(D * j + 512 * c, 128), 640)
        return pltpu.make_async_copy(wqkv_s.at[:, cols], stage.at[j % 2], stage_sem.at[j % 2])

    def piece(i, slot):
        cols = pl.ds(pl.multiple_of(384 * i, 128), 384)
        return pltpu.make_async_copy(wqkv_t.at[:, cols], stage.at[slot, :, pl.ds(0, 384)], stage_sem.at[slot])

    window(0).start()
    window(1).start()
    for copy in out_w:
        copy.start()

    def remote(src, dst, send, recv, to):
        return pltpu.make_async_remote_copy(
            src_ref=src, dst_ref=dst, send_sem=send, recv_sem=recv, device_id=to, device_id_type=MESH
        )

    def slot(dx):
        return hb.at[2 * dx + t]

    to_right = remote(slot(0), slot(3), ss.at[0], ro.at[3], right)
    to_left = remote(slot(0), slot(1), ss.at[1], ro.at[1], left)
    to_sib = [remote(slot(dx), slot(dx), ss.at[2 + dx], rb.at[dx], sib) for dx in range(4)]
    on_left = remote(slot(1).at[0], slot(2).at[0], ss.at[6], ro.at[2], left)
    on_right = remote(slot(3).at[1], slot(2).at[1], ss.at[7], ro.at[4], right)
    swaps = [
        remote(hb.at[8, :, pl.ds(64 * q, 64)], hb.at[1, :, pl.ds(64 * q, 64)], sw_s.at[q], sw_r.at[q], partner)
        for q in range(4)
    ]
    swap_z = remote(z_ref, zb.at[0], ss.at[8], rz.at[0], partner)
    swap_dz = remote(dz_ref, zb.at[1], ss.at[9], rz.at[1], partner)

    own = 8 * t
    for copy in zin_copies:
        copy.wait()
    for q in range(4):

        def put(at_row, rows, h, dh):
            hb[own, 0, pl.ds(64 * q + at_row, rows), :] = h
            hb[own, 1, pl.ds(64 * q + at_row, rows), :] = dh

        normed_hidden(
            64,
            lambda a, n: z_ref[pl.ds(64 * q + a, n), :],
            lambda a, n: dz_ref[pl.ds(64 * q + a, n), :],
            mod_ref, dmod_ref, put,
        )
        if q == 0:
            pl.when(same)(lambda: pl.semaphore_wait(barrier, 7))
            pl.when(moved)(lambda: pl.semaphore_wait(barrier, 8))
        pl.when(moved)(swaps[q].start)

    @pl.when(same)
    def _():
        to_sib[0].start()
        to_right.start()
        to_left.start()
        zb[0] = z_ref[...]
        zb[1] = dz_ref[...]

    tell(0)

    for j in range(3):
        window(j).wait()
        for i in range(5):
            wtmp[pl.ds(128 * i, 128), :] = stage[j % 2, :, pl.ds(128 * i, 128)].T
        if j == 0:
            window(2).start()
        else:
            piece(j - 1, j % 2).start()
        wt[pl.ds(576 * j, 576), :] = wtmp[pl.ds(pl.multiple_of(64 * c, 64), 576), :]

    hear(0)
    tell(1)

    for i, g in enumerate((qg_s, kg_s, qg_t, kg_t)):
        rows = lax.broadcasted_iota(jnp.int32, (HD, HD), 0)
        cols = lax.broadcasted_iota(jnp.int32, (HD, HD), 1)
        gains[i] = jnp.sum(jnp.where(rows == cols, g[...], 0.0), 1, keepdims=True)

    acc[...] = jnp.zeros_like(acc)
    mx[...] = jnp.full_like(mx, -1e30)

    def turn_piece(i, _):
        which = lax.rem(i + 1, 2)
        piece(i, which).wait()
        for n in range(3):
            rows = pl.ds(pl.multiple_of(384 * i + 128 * n, 128), 128)
            wtt[rows, :] = stage[which, :, pl.ds(128 * n, 128)].T

        @pl.when(i < 7)
        def _():
            piece(i + 2, which).start()

        return 0

    lax.fori_loop(0, 9, turn_piece, 0)
    hear(1)
    tell(2)

    def query_rows(part):
        kt[0:576, 0:512] = dot(wt[0:576, :], hb[part].reshape(2 * TOK, D), ((1,), (1,)))

        def make_query(h, _):
            rows = pl.ds(pl.multiple_of(h * HD, 8), HD)
            first, second = query_operands(kt[rows, 0:256], kt[rows, 256:512], gains[0])
            for q in range(2):
                to = slice(256 * q + 128 * part, 256 * q + 128 * part + 128)
                qs[h, :, to] = first[:, 128 * q : 128 * q + 128]
                qd[h, :, to] = second[:, 128 * q : 128 * q + 128]
            return 0

        lax.fori_loop(0, HALF, make_query, 0, unroll=4)

    pl.when(moved)(to_sib[0].wait_recv)
    query_rows(0)

    @pl.when(moved)
    def _():
        for copy in swaps:
            copy.wait_recv()
        to_sib[0].start()
        to_right.start()
        to_left.start()
        swap_z.start()
        swap_dz.start()

    @pl.when(same)
    def _():
        to_left.wait_recv()
        to_sib[1].start()
        to_right.wait_recv()
        to_sib[3].start()
        to_sib[0].wait_recv()

    query_rows(1)
    hear(2)
    pl.semaphore_signal(relay.at[3], inc=1, device_id=sib, device_id_type=MESH)

    def keys_of(index, s):
        kt[:, 512 * s : 512 * s + 512] = dot(wt[576:1728, :], hb[index].reshape(2 * TOK, D), ((1,), (1,)))

    def prepare(h):
        krow = pl.ds(pl.multiple_of(h * HD, 8), HD)
        vrow = pl.ds(pl.multiple_of(576 + h * HD, 8), HD)
        for s in range(2):
            o = 512 * s
            keys = slice(256 * s, 256 * s + 256)
            kds[h, keys, :] = key_operand(kt[krow, o : o + 256], kt[krow, o + 256 : o + 512], gains[1])
            ve, vg = value_operands(kt[vrow, o : o + 256], kt[vrow, o + 256 : o + 512])
            ves[h, :, keys] = ve
            vgs[h, :, keys] = vg

    def attend(h, cols):
        kd = kds[h]
        s = dot(kd, qs[h, :, cols], ((1,), (0,)))
        ds = dot(kd, qd[h, :, cols], ((1,), (0,)))
        old = mx[h, 0:1, cols]
        new = jnp.maximum(old, jnp.max(s, 0, keepdims=True))
        mx[h, 0:1, cols] = new
        e = jnp.exp2(s - new)
        g = e * ds
        keep = jnp.exp2(old - new)
        of_e = dot(ves[h], e.astype(BF16), ((1,), (0,)))
        of_g = dot(vgs[h], g.astype(BF16), ((1,), (0,)))
        acc[h, 0:72, cols] = acc[h, 0:72, cols] * keep + of_e[0:72]
        acc[h, 72:152, cols] = acc[h, 72:152, cols] * keep + of_e[72:152] + of_g

    def heads(start, stop, cols, with_keys):
        def one_head(h, _):
            if with_keys:
                prepare(h)
            attend(h, cols)
            return 0

        lax.fori_loop(start, stop, one_head, 0, unroll=stop - start)

    def two_shards(i, _):
        @pl.when((i == 1) & same)
        def _():
            on_left.start()
            on_right.start()

        @pl.when((i == 1) & moved)
        def _():
            to_sib[1].wait_recv()
            to_sib[3].wait_recv()

        @pl.when((i == 2) & moved)
        def _():
            to_left.wait_recv()
            on_left.start()
            to_sib[1].start()
            to_right.wait_recv()
            on_right.start()
            to_sib[3].start()

        @pl.when((i == 2) & same)
        def _():
            on_left.wait_recv()
            on_right.wait_recv()
            to_sib[2].start()
            to_sib[1].wait_recv()
            to_sib[3].wait_recv()

        keys_of(jnp.where(i == 0, 0, i + 1), 0)
        keys_of(jnp.where(i == 0, 1, i + 5), 1)
        heads(0, HALF, slice(0, 512), True)
        return 0

    lax.fori_loop(0, 3, two_shards, 0)

    @pl.when(moved)
    def _():
        on_left.wait_recv()
        on_right.wait_recv()
        to_sib[2].start()

    to_sib[2].wait_recv()
    keys_of(4, 0)
    keys_of(5, 1)
    heads(0, HALF, slice(0, 256), True)

    trades = [remote(mine.at[1, q], theirs.at[q], tr_s.at[q], tr_r.at[q], sib) for q in range(2)]

    def finish(q):
        def finish_head(h, _):
            attn, dattn = normalised(acc[h, :, 256 * q : 256 * q + 256])
            rows = pl.ds(pl.multiple_of(h * HD, 8), HD)
            for part in range(2):
                at[part, q, rows, 0:128] = attn[:, 128 * part : 128 * part + 128]
                at[part, q, rows, 128:256] = dattn[:, 128 * part : 128 * part + 128]
            return 0

        lax.fori_loop(0, HALF, finish_head, 0, unroll=4)
        mine[1, q] = at[1 - t, q].astype(BF16)
        trades[q].start()
        mine[0, q] = at[t, q].astype(BF16)

    lo = pl.ds(pl.multiple_of(576 * c, 16), 576)
    hi = pl.ds(pl.multiple_of(576 * (1 - c), 16), 576)

    def forward(q, n):
        a, b, d = OFFSETS[n]
        to = (lax.rem(zh + a, 2), lax.rem(y + b, 4), c, lax.rem(zl + d, 2), x)
        return remote(
            tx.at[q, member(to[0], to[1], to[3])], rx.at[q, me], fs.at[16 * q + n], fr.at[16 * q + n], to
        )

    def forward_own(q):
        return pltpu.make_async_copy(tx.at[q, me], rx.at[q, me], fl.at[q])

    def give_back(q, n):
        a, b, d = OFFSETS[n]
        z2, y2, l2 = lax.rem(zh + a, 2), lax.rem(y + b, 4), lax.rem(zl + d, 2)
        return remote(
            ty.at[q, member(z2, y2, l2)], got.at[q, me], gs.at[16 * q + n], gr.at[16 * q + n], (z2, y2, l2, c, x)
        )

    def give_own(q):
        return pltpu.make_async_copy(ty.at[q, me], got.at[q, me], gl.at[q])

    others = [n for n in range(16) if n != SELF]
    gate = mod_ref[2:3, :]
    dgate = dmod_ref[2:3, :]

    def spatial_out(q):
        both = dot(mine[0, q], wos[lo, :], ((0,), (0,)))
        trades[q].wait_recv()
        both += dot(theirs[q], wos[hi, :], ((0,), (0,)))
        rows = pl.ds(CHUNK * q, CHUNK)
        proj, dproj = both[0:CHUNK], both[CHUNK:]
        tx[q] = joined(
            zb[0, rows, :].astype(F32) + gate * proj,
            zb[1, rows, :].astype(F32) + gate * dproj + dgate * proj,
        )

    def send(q):
        forward_own(q).start()
        for n in others:
            forward(q, n).start()

    finish(0)
    heads(0, 4, slice(256, 512), False)
    out_w[0].wait()
    out_w[1].wait()

    @pl.when(moved)
    def _():
        swap_z.wait_recv()
        swap_dz.wait_recv()

    pl.semaphore_wait(relay.at[3], 1)
    spatial_out(0)
    send(0)
    heads(4, HALF, slice(256, 512), False)
    finish(1)
    spatial_out(1)
    for n in others:
        forward(0, n).wait_send()
    send(1)

    ki = lax.broadcasted_iota(jnp.int32, (CHUNK, CHUNK), 0)
    qi = lax.broadcasted_iota(jnp.int32, (CHUNK, CHUNK), 1)
    place = (ki & 7) == (qi & 7)

    def temporal_chunk(q, _):
        forward_own(q).wait()
        for n in others:
            forward(q, n).wait_recv()

        def put(at_row, rows, h, dh):
            th[pl.ds(at_row, rows), :] = h
            th[pl.ds(CHUNK + at_row, rows), :] = dh

        def half(which):
            return lambda a, n: both_halves(rx[q, pl.ds(a // 8, n // 8)].astype(F32))[which]

        normed_hidden(CHUNK, half(0), half(1), mod_ref, dmod_ref, put)
        for j in range(3):
            kt[:, 256 * j : 256 * j + 256] = dot(wtt[D * j : D * j + D, :], th[...], ((1,), (1,)))

        def one_head(h, _):
            rows = pl.ds(pl.multiple_of(h * HD, 8), HD)
            first, second = query_operands(kt[rows, 0:128], kt[rows, 128:256], gains[2])
            kd = key_operand(kt[rows, 256:384], kt[rows, 384:512], gains[3])
            ve = value_operands(kt[rows, 512:640], kt[rows, 640:768])[0]
            both = dot(kd, jnp.concatenate([first, second], 1), ((1,), (0,)))
            s = jnp.where(place, both[:, 0:128], -1e30)
            e = jnp.exp2(s - jnp.max(s, 0, keepdims=True))
            g = e * both[:, 128:256]
            sums = dot(ve, jnp.concatenate([e, g], 1).astype(BF16), ((1,), (0,)))
            of_e, of_g = sums[:, 0:128], sums[:, 128:256]
            inv = 1.0 / of_e[144:145]
            attn = of_e[0:72] * inv
            dattn = (of_e[72:144] + of_g[0:72] - of_g[144:145] * attn) * inv
            to_rows = pl.ds(pl.multiple_of(lax.rem(h, 8) * HD, 8), HD)
            at[0, h // 8, to_rows, 0:128] = attn
            at[0, h // 8, to_rows, 128:256] = dattn
            return 0

        lax.fori_loop(0, HEADS, one_head, 0, unroll=4)
        both = dot(at[0, 0].astype(BF16), wot[0:576, :], ((0,), (0,)))
        both += dot(at[0, 1].astype(BF16), wot[576:1152, :], ((0,), (0,)))
        proj, dproj = both[0:CHUNK], both[CHUNK:]
        z, dz = both_halves(rx[q].astype(F32))
        ty[q] = joined(z + gate * proj, dz + gate * dproj + dgate * proj)
        pl.when(same)(lambda: give_own(q).start())
        pl.when(moved)(lambda: give_back(q, SELF).start())
        for n in others:
            give_back(q, n).start()
        return 0

    lax.fori_loop(0, 2, temporal_chunk, 0)

    def collect(q, _):
        pl.when(same)(lambda: give_own(q).wait())
        pl.when(moved)(lambda: give_back(q, SELF).wait())
        for n in others:
            give_back(q, n).wait()
        return 0

    lax.fori_loop(0, 2, collect, 0)

    for n in others:
        forward(1, n).wait_send()
    for copy in (to_right, to_left, *to_sib, on_left, on_right, *trades):
        copy.wait_send()

    @pl.when(moved)
    def _():
        for copy in (*swaps, swap_z, swap_dz):
            copy.wait_send()


def split_kernel(both_ref, out_ref, dout_ref):
    for q in range(2):
        z, dz = both_halves(both_ref[q].astype(F32))
        out_ref[CHUNK * q : CHUNK * (q + 1), :] = z.astype(BF16)
        dout_ref[CHUNK * q : CHUNK * (q + 1), :] = dz.astype(BF16)


def body(
    latent,
    latent_tangent,
    modulation,
    modulation_tangent,
    w_qkv_s,
    w_out_s,
    q_gain_s,
    k_gain_s,
    w_qkv_t,
    w_out_t,
    q_gain_t,
    k_gain_t,
):
    shape = latent.shape
    vmem = pl.BlockSpec(memory_space=pltpu.VMEM)
    hbm = pl.BlockSpec(memory_space=pl.ANY)
    dma = pltpu.SemaphoreType.DMA
    one = jax.ShapeDtypeStruct((TOK, D), BF16)
    row = lambda gain: gain.reshape(1, HD)
    both = pl.pallas_call(
        block_kernel,
        out_shape=jax.ShapeDtypeStruct((2, 16, 16, D), BF16),
        in_specs=[hbm, hbm, vmem, vmem, hbm, hbm, vmem, vmem, hbm, hbm, vmem, vmem],
        out_specs=vmem,
        scratch_shapes=[
            pltpu.VMEM((2, TOK, D), BF16),
            pltpu.VMEM((9, 2, TOK, D), BF16),
            pltpu.VMEM((2, TOK, D), BF16),
            pltpu.VMEM((2, D, 640), BF16),
            pltpu.VMEM((640, D), BF16),
            pltpu.VMEM((1728, D), BF16),
            pltpu.VMEM((D, D), BF16),
            pltpu.VMEM((3 * D, D), BF16),
            pltpu.VMEM((D, D), BF16),
            pltpu.VMEM((D, 4 * TOK), F32),
            pltpu.VMEM((HALF, 144, 2 * TOK), BF16),
            pltpu.VMEM((HALF, 144, 2 * TOK), BF16),
            pltpu.VMEM((HALF, 2 * TOK, 144), BF16),
            pltpu.VMEM((HALF, 160, 2 * TOK), BF16),
            pltpu.VMEM((HALF, 80, 2 * TOK), BF16),
            pltpu.VMEM((HALF, 160, 2 * TOK), F32),
            pltpu.VMEM((HALF, 8, 2 * TOK), F32),
            pltpu.VMEM((2, 2, 576, TOK), F32),
            pltpu.VMEM((2, 2, 576, TOK), BF16),
            pltpu.VMEM((2, 576, TOK), BF16),
            pltpu.VMEM((TOK, D), BF16),
            pltpu.VMEM((2, 16, 16, D), BF16),
            pltpu.VMEM((2, 16, 16, D), BF16),
            pltpu.VMEM((2, 16, 16, D), BF16),
            pltpu.VMEM((4, HD, 1), F32),
            pltpu.SemaphoreType.REGULAR((4,)),
            dma((2,)), dma((2,)), dma((2,)), dma((5,)), dma((4,)), dma((2,)), dma((2,)), dma((2,)), dma((10,)),
            dma((4,)), dma((4,)),
            dma((32,)), dma((32,)), dma((2,)), dma((32,)), dma((32,)), dma((2,)),
        ],
        compiler_params=pltpu.CompilerParams(
            collective_id=1, has_side_effects=True, vmem_limit_bytes=63 * 2**20
        ),
        cost_estimate=pl.CostEstimate(flops=53_000_000_000, bytes_accessed=25_000_000, transcendentals=9_000_000),
        name="blocks",
    )(
        latent.reshape(TOK, D), latent_tangent.reshape(TOK, D), modulation, modulation_tangent,
        w_qkv_s, w_out_s, row(q_gain_s), row(k_gain_s), w_qkv_t, w_out_t, row(q_gain_t), row(k_gain_t),
    )
    out, dout = pl.pallas_call(
        split_kernel,
        out_shape=(one, one),
        in_specs=[vmem],
        out_specs=(vmem, vmem),
        name="results",
    )(both)
    return out.reshape(shape), dout.reshape(shape)


def solution(mesh):
    split = Mesh(mesh.devices.reshape(2, 4, 2, 2, 4), AXES)
    tokens = P(("zh", "y", "core"), ("zl", "x"), None, None)
    return jax.shard_map(
        body, mesh=split, in_specs=(tokens, tokens) + (P(),) * 10, out_specs=(tokens, tokens), check_vma=False
    )
```
